128 devices in a mesh: section: 2 (over core), dp: 64 (over x, y, z).
Axes of the slice: x: 4, y: 4, z: 4, core: 2. Of those that a mesh axis runs over, the one named last changes fastest.
Arguments:
- boundary: bfloat16 [2, 2, 8192, 960], P('section', None, 'dp'), may hold values from -6 to 6
- lengths: int32 [2, 64], P(None, 'dp'), may hold values from 32 to 128, as said below
- gain_attn: bfloat16 [2, 960], P('section', 'dp'), may hold values from 0.099609375 to 1.8984375
- w_query: bfloat16 [2, 960, 960], P('section', 'dp'), may hold values from -0.1875 to 0.1875
- w_key: bfloat16 [2, 960, 320], P('section', 'dp'), may hold values from -0.1875 to 0.1875
- w_value: bfloat16 [2, 960, 320], P('section', 'dp'), may hold values from -0.1875 to 0.1875
- w_out: bfloat16 [2, 960, 960], P('section', None, 'dp'), may hold values from -1.5 to 1.5
- gain_mlp: bfloat16 [2, 960], P('section', 'dp'), may hold values from 0.099609375 to 1.8984375
- w_gate: bfloat16 [2, 960, 2560], P('section', 'dp'), may hold values from -0.1875 to 0.1875
- w_up: bfloat16 [2, 960, 2560], P('section', 'dp'), may hold values from -0.1875 to 0.1875
- w_down: bfloat16 [2, 2560, 960], P('section', None, 'dp'), may hold values from -0.125 to 0.125
Outputs:
- ends_out: float32 [2, 2, 8192, 960], P('section', None, 'dp')
- grad_gain_attn: float32 [2, 960], P('section', 'dp')
- grad_w_query: float32 [2, 960, 960], P('section', 'dp')
- grad_w_key: float32 [2, 960, 320], P('section', 'dp')
- grad_w_value: float32 [2, 960, 320], P('section', 'dp')
- grad_w_out: float32 [2, 960, 960], P('section', None, 'dp')
- grad_gain_mlp: float32 [2, 960], P('section', 'dp')
- grad_w_gate: float32 [2, 960, 2560], P('section', 'dp')
- grad_w_up: float32 [2, 960, 2560], P('section', 'dp')
- grad_w_down: float32 [2, 2560, 960], P('section', None, 'dp')
The draws below stay inside these ranges and needn't reach their ends.
Inputs may be any that keep to these rules, and one draw needn't show every extreme that they name: lengths[m, s] is the number of valid leading tokens of sequence s of micro-batch m; each micro-batch has at least one sequence of full length 128.
All inputs are finite; a program needn't handle non-finite values.
Results may differ from the reference program's by a relative error of at most 0.03.
Values may be sent and summed in bfloat16 or wider, within the bound.
A program may use at most 256 MiB of HBM per device.

```python
import jax
import jax.numpy as jnp
from jax import lax

D = 960
HQ = 15
KV = 5
HD = 64
FF = 2560
SEQ = 128
MICRO = 2
TOKENS = 8192


def draw_lengths(key, part):
    key = jax.random.fold_in(key, 7)
    first_key, second_key = jax.random.split(key)
    seq_count = TOKENS // SEQ
    drawn = jax.random.randint(first_key, (MICRO, seq_count), SEQ // 4, SEQ + 1)
    chosen = jax.random.randint(second_key, (MICRO, 1), 0, seq_count)
    columns = jnp.arange(seq_count)[None, :]
    return jnp.where(columns == chosen, SEQ, drawn).astype(jnp.int32)


def levels(key, shape, cuts, smallest, high):
    level = 1.0
    for axis_at, parts in cuts:
        draws = jax.random.uniform(jax.random.fold_in(jax.random.fold_in(key, 6), axis_at), (parts,), jnp.float32, smallest / len(cuts), high / len(cuts))
        level = level * jnp.repeat(jnp.exp(draws), shape[axis_at] // parts).reshape((-1,) + (1,) * (len(shape) - 1 - axis_at))
    return level


def centred(rng, extent, deviation, bound, cuts=(), held_as=jnp.bfloat16):
    loudness = levels(rng, extent, cuts, -0.22, 0.18) if cuts else 1.0
    values = jax.random.normal(rng, extent, jnp.float32) * deviation * loudness
    return jnp.minimum(jnp.maximum(values, -bound), bound).astype(held_as)


def setup_inputs(seed: int = 0) -> dict:
    streams_of = jax.random.split(jax.random.key(seed), 12)
    return {
        "boundary": centred(streams_of[0], (2, MICRO, TOKENS, D), 1.0, 6.0, ((0, 2), (2, 64))),
        "lengths": draw_lengths(jax.random.fold_in(streams_of[11], 71), 0),
        "gain_attn": jnp.clip(1.0 + 0.18 * jax.random.normal(streams_of[2], (2, D), jnp.float32), 0.099609375, 1.8984375).astype(jnp.bfloat16),
        "w_query": centred(streams_of[3], (2, D, HQ * HD), D ** -0.5, 0.1875, ((0, 2), (1, 64))),
        "w_key": centred(streams_of[4], (2, D, KV * HD), D ** -0.5, 0.1875, ((0, 2), (1, 64))),
        "w_value": centred(streams_of[5], (2, D, KV * HD), D ** -0.5, 0.1875, ((0, 2), (1, 64))),
        "w_out": centred(streams_of[6], (2, HQ * HD, D), (max(1, 2 * HQ * HD // SEQ)) ** -0.5, 1.5, ((0, 2), (2, 64))),
        "gain_mlp": jnp.clip(1.0 + 0.18 * jax.random.normal(streams_of[7], (2, D), jnp.float32), 0.099609375, 1.8984375).astype(jnp.bfloat16),
        "w_gate": centred(streams_of[8], (2, D, FF), D ** -0.5, 0.1875, ((0, 2), (1, 64))),
        "w_up": centred(streams_of[9], (2, D, FF), D ** -0.5, 0.1875, ((0, 2), (1, 64))),
        "w_down": centred(streams_of[10], (2, FF, D), FF ** -0.5, 0.125, ((0, 2), (2, 64))),
    }


EPS = 1e-05
NEG = -1e+30
BASE = 10000.0
HIGH = lax.Precision.HIGHEST

@jax.custom_vjp
def low(v):
    return lax.optimization_barrier(v.astype(jnp.bfloat16)).astype(jnp.float32)

@jax.custom_vjp
def low_back(v):
    return v

def low_keep(v):
    return (low(v), None)

def low_pass(kept, grad):
    return (grad,)

def back_keep(v):
    return (v, None)

def back_low(kept, grad):
    return (low(grad),)
low.defvjp(low_keep, low_pass)
low_back.defvjp(back_keep, back_low)

def tables(seq_len):
    halfway = HD // 2
    frequency = BASE ** (-(jnp.arange(halfway, dtype=jnp.float32) * 2.0 / HD))
    angles = jnp.arange(seq_len, dtype=jnp.float32)[:, None] * frequency[None, :]
    return (jnp.cos(angles), jnp.sin(angles))

def rotate(vectors, cosine_table, sine_table):
    halfway = vectors.shape[-1] // 2
    first_half = vectors[..., :halfway]
    second_half = vectors[..., halfway:]
    cosine_cols = cosine_table[:, None, :]
    sine_cols = sine_table[:, None, :]
    return jnp.concatenate([first_half * cosine_cols - second_half * sine_cols, second_half * cosine_cols + first_half * sine_cols], axis=-1)

def rms_scale(matrix, gain):
    return matrix * lax.rsqrt(lax.optimization_barrier(jnp.mean(matrix * matrix, axis=-1, keepdims=True)) + EPS) * gain

def attention(queries, keys, values, length):
    seq_len = queries.shape[0]
    grouped = queries.reshape(seq_len, KV, HQ // KV, HD)
    scores = low_back(jnp.einsum('ihgd,jhd->hgij', grouped, keys, precision=HIGH) * HD ** (-0.5))
    row_pos = jnp.arange(seq_len, dtype=jnp.int32)[:, None]
    col_pos = jnp.arange(seq_len, dtype=jnp.int32)[None, :]
    allowed = (col_pos <= row_pos) & (col_pos < length)
    probs = low(jax.nn.softmax(jnp.where(allowed, scores, NEG), axis=-1))
    mixed = jnp.einsum('hgij,jhd->ihgd', probs, values, precision=HIGH)
    return mixed.reshape(seq_len, HQ * HD)

def layer(matrix, length, params):
    gain_one, w_query, w_key, w_value, w_out, gain_two, w_gate, w_up, w_down = params
    seq_len = matrix.shape[0]
    cosine_table, sine_table = tables(seq_len)
    normed_one = low(rms_scale(matrix, gain_one))
    query_pre = low_back(jnp.dot(normed_one, w_query, precision=HIGH))
    key_pre = low_back(jnp.dot(normed_one, w_key, precision=HIGH))
    values = low_back(low(jnp.dot(normed_one, w_value, precision=HIGH)))
    queries = low(rotate(query_pre.reshape(seq_len, HQ, HD), cosine_table, sine_table))
    keys = low(rotate(key_pre.reshape(seq_len, KV, HD), cosine_table, sine_table))
    mixed = low_back(low(attention(queries, keys, values.reshape(seq_len, KV, HD), length)))
    resid = matrix + low_back(jnp.dot(mixed, w_out, precision=HIGH))
    normed_two = low(rms_scale(resid, gain_two))
    gate = low_back(jnp.dot(normed_two, w_gate, precision=HIGH))
    upper = low_back(jnp.dot(normed_two, w_up, precision=HIGH))
    hidden = low(jax.nn.silu(gate) * upper)
    return resid + low_back(jnp.dot(hidden, w_down, precision=HIGH))

def reference(boundary, lengths, gain_attn, w_query, w_key, w_value, w_out, gain_mlp, w_gate, w_up, w_down):
    params = tuple((weight.astype(jnp.float32) for weight in (gain_attn, w_query, w_key, w_value, w_out, gain_mlp, w_gate, w_up, w_down)))
    micro_count = boundary.shape[1]
    seq_count = lengths.shape[1]
    seq_len = boundary.shape[2] // seq_count
    inputs = boundary[0].astype(jnp.float32).reshape(micro_count * seq_count, seq_len, boundary.shape[3])
    cotangent = boundary[1].astype(jnp.float32).reshape(micro_count * seq_count, seq_len, boundary.shape[3])
    flat_lengths = lengths.reshape(-1).astype(jnp.int32)

    def forward(inputs, params):
        first_layer = tuple((weight[0] for weight in params))
        second_layer = tuple((weight[1] for weight in params))

        def run_pair(matrix, length):
            middle = low_back(low(layer(matrix, length, first_layer)))
            return layer(middle, length, second_layer)

        def scan_step(carry, item):
            return (carry, jax.checkpoint(run_pair)(item[0], item[1]))
        _, outputs = lax.scan(scan_step, jnp.zeros((), jnp.float32), (inputs, flat_lengths))
        return outputs
    outputs, pullback = jax.vjp(forward, inputs, params)
    grad_inputs, grad_params = pullback(cotangent)
    ends = jnp.stack([grad_inputs, outputs]).reshape(boundary.shape)
    return (ends, grad_params[0], grad_params[1], grad_params[2], grad_params[3], grad_params[4], grad_params[5], grad_params[6], grad_params[7], grad_params[8])
```

```python
import numpy as np

import jax
import jax.numpy as jnp
from jax import lax
from jax.experimental import pallas as pl
from jax.experimental.pallas import tpu as pltpu
from jax.sharding import PartitionSpec as P

D = 960
DP = 1024
HQ = 15
KV = 5
GROUP = HQ // KV
HD = 64
FF = 2560
SEQ = 128
MICRO = 2
ROWS = MICRO * SEQ
RING = 4
SHARD = 15
PADDED = 16
EPS = 1e-05
NEG = -1e30
BASE = 10000.0
BF = jnp.bfloat16
F32 = jnp.float32
MESH = pl.DeviceIdType.MESH

C_Q = 0
C_O = 1024
C_KV = 2048
C_G = 2688
C_U = 5248
C_D = 7808
C_ALL = 10368
CHUNK = 512
CHUNKS = FF // CHUNK

STRIDES = (16, 4, 1)
ORDERS = ((0, 1, 2), (1, 2, 0), (2, 0, 1))


def make_pieces():
    pieces = []
    for start, tiles in ((C_D, (7, 7, 6)), (C_G, (13, 13, 14)), (C_Q, (7, 7, 7))):
        at = start
        for part, count in enumerate(tiles):
            left = (count + 1) // 2 if part != 1 else count // 2
            pieces.append((at, at + 128 * left, at + 128 * count, ORDERS[part]))
            at += 128 * count
    return pieces


PIECES = make_pieces()


def position():
    me = lax.axis_index("dp")
    return me, (me // 16, (me // 4) % 4, me % 4)


def neighbour(me, coords, axis, step):
    here = coords[axis]
    return me + ((here + step) % RING - here) * STRIDES[axis]


def block(ref, order, phase, coords, at, first, last, later_full):
    index = [None, None, None]
    for place, axis in enumerate(order):
        if place == phase:
            index[axis] = at
        elif (place > phase) == later_full:
            index[axis] = slice(None)
        else:
            index[axis] = coords[axis]
    return ref.at[index[0], index[1], index[2], :, first:last]


def remote(src, dst, send, recv, device):
    return pltpu.make_async_remote_copy(
        src_ref=src,
        dst_ref=dst,
        send_sem=send,
        recv_sem=recv,
        device_id={"dp": device},
        device_id_type=MESH,
    )


class Gather:
    def __init__(self, number, whole, send, recv, me, coords):
        self.first, self.mid, self.last, self.order = PIECES[number]
        self.whole, self.send, self.recv = whole, send.at[number], recv.at[number]
        self.me, self.coords = me, coords
        self.copies = []
        self.pending = []

    def go(self, phase, slot, at, first, last, step):
        axis = self.order[phase]
        view = block(self.whole, self.order, phase, self.coords, at, first, last, False)
        index = phase * 4 + slot
        copy = remote(
            view,
            view,
            self.send.at[index],
            self.recv.at[index],
            neighbour(self.me, self.coords, axis, step),
        )
        copy.start()
        self.copies.append(copy)
        return copy

    def step(self, number):
        phase, second = divmod(number, 2)
        for copy in self.pending:
            copy.wait_recv()
        self.pending = []
        if phase == 3:
            return
        here = self.coords[self.order[phase]]
        if not second:
            right = self.go(phase, 0, here, self.first, self.last, 1)
            left = self.go(phase, 1, here, self.first, self.last, -1)
        else:
            right = self.go(phase, 2, (here + 3) % RING, self.first, self.mid, 1)
            left = self.go(phase, 3, (here + 1) % RING, self.mid, self.last, -1)
        self.pending = [right, left]

    def finish(self):
        for copy in self.copies:
            copy.wait_send()


class Scatter:
    def __init__(self, number, whole, lands, send, recv, result, me, coords):
        self.first, self.mid, self.last, self.order = PIECES[number]
        self.whole, self.lands = whole, lands
        self.send, self.recv = send.at[number], recv.at[number]
        self.result = result
        self.me, self.coords = me, coords
        self.copies = []
        self.now = {}

    def view(self, phase, at, side):
        first, last = (self.first, self.mid) if side == 0 else (self.mid, self.last)
        return block(self.whole, self.order, phase, self.coords, at, first, last, True)

    def go(self, phase, slot, at, side, step):
        copy = remote(
            self.view(phase, at, side),
            self.lands[phase][side].at[slot],
            self.send.at[phase * 6 + side * 3 + slot],
            self.recv.at[phase * 6 + side * 3 + slot],
            neighbour(self.me, self.coords, self.order[phase], step),
        )
        copy.start()
        self.copies.append(copy)
        self.now[side, slot] = copy

    def add(self, phase, at, side, slots):
        view = self.view(phase, at, side)
        land = self.lands[phase][side]
        if phase == 2:
            total = view[...].astype(F32)
            for slot in slots:
                total = total + land[slot].astype(F32)
            if len(slots) == 2:
                first, last = (self.first, self.mid) if side == 0 else (self.mid, self.last)
                self.result[:, first:last] = total
            else:
                view[...] = total.astype(BF)
            return

        def one(step, carry):
            total = view[step].astype(F32)
            for slot in slots:
                total = total + land[slot, step].astype(F32)
            view[step] = total.astype(BF)
            return carry

        lax.fori_loop(0, RING, one, 0)

    def step(self, number):
        phase, part = divmod(number, 3)
        if phase == 3:
            return
        here = self.coords[self.order[phase]]
        ahead, across, behind = (here + 1) % RING, (here + 2) % RING, (here + 3) % RING
        if part == 0:
            self.go(phase, 0, across, 0, 1)
            self.go(phase, 0, across, 1, -1)
            self.go(phase, 1, ahead, 1, 1)
            self.go(phase, 1, behind, 0, -1)
        elif part == 1:
            self.now[0, 0].wait_recv()
            self.add(phase, ahead, 0, (0,))
            self.go(phase, 2, ahead, 0, 1)
            self.now[1, 0].wait_recv()
            self.add(phase, behind, 1, (0,))
            self.go(phase, 2, behind, 1, -1)
        else:
            for side in (0, 1):
                self.now[side, 1].wait_recv()
                self.now[side, 2].wait_recv()
                self.add(phase, here, side, (1, 2))

    def finish(self):
        for copy in self.copies:
            copy.wait_send()


def dot(left, right):
    return jnp.dot(left, right, preferred_element_type=F32)


def dot_nt(left, right):
    return lax.dot_general(left, right, (((1,), (1,)), ((), ())), preferred_element_type=F32)


def dot_tn(left, right):
    return lax.dot_general(left, right, (((0,), (0,)), ((), ())), preferred_element_type=F32)


def columns(whole, first, count):
    return whole[:, :, :, :, pl.ds(first, count)].reshape(DP, count)


def swap_halves(tile):
    lane = lax.broadcasted_iota(jnp.int32, tile.shape, 1)
    return jnp.where(lane % HD < HD // 2, pltpu.roll(tile, 96, 1), pltpu.roll(tile, 32, 1))


def norm_forward(matrix, gain):
    scale = lax.rsqrt(jnp.sum(matrix * matrix, axis=1, keepdims=True) * (1.0 / D) + EPS)
    return (matrix * scale * gain).astype(BF)


def norm_backward(matrix, gain, grad):
    scale = lax.rsqrt(jnp.sum(matrix * matrix, axis=1, keepdims=True) * (1.0 / D) + EPS)
    scaled = grad * gain
    inner = jnp.sum(scaled * matrix, axis=1, keepdims=True) * (1.0 / D)
    grad_matrix = scale * (scaled - matrix * (scale * scale * inner))
    grad_gain = jnp.sum(grad * matrix * scale, axis=0, keepdims=True)
    return grad_matrix, grad_gain


def kernel(
    shard,
    rows_in,
    lengths,
    cosine,
    sine,
    ends,
    result,
    whole,
    entering,
    grad_out,
    crossing,
    spread,
    normed_one,
    queries,
    key_value,
    probs,
    mixed,
    resid,
    normed_two,
    gate_up,
    hidden,
    total,
    grad_resid,
    grad_branch,
    grad_mixed,
    grad_kv,
    gains,
    grad_gains,
    gather_send,
    gather_recv,
    scatter_send,
    scatter_recv,
    cross_send,
    cross_recv,
    *lands,
):
    section = lax.axis_index("section")
    me, coords = position()
    is_first = section == 0

    barrier = pltpu.get_barrier_semaphore()
    for axis in range(3):
        for step in (1, -1):
            pl.semaphore_signal(
                barrier,
                inc=1,
                device_id={"dp": neighbour(me, coords, axis, step)},
                device_id_type=MESH,
            )
    pl.semaphore_signal(barrier, inc=1, device_id={"section": 1 - section}, device_id_type=MESH)
    whole[coords[0], coords[1], coords[2]] = shard[...]
    pl.semaphore_wait(barrier, 7)

    gathers = [
        Gather(number, whole, gather_send, gather_recv, me, coords)
        for number in range(len(PIECES))
    ]
    order = (6, 7, 8, 3, 4, 5, 0, 1, 2)
    for number in order:
        gathers[number].step(0)

    row = lax.broadcasted_iota(jnp.int32, (D, DP), 0)
    column = lax.broadcasted_iota(jnp.int32, (D, DP), 1)
    chosen = (column - column // PADDED == row) & (column % PADDED != SHARD)
    spread[...] = jnp.where(chosen, 1.0, 0.0).astype(BF)
    own_rows = dot(rows_in[...], spread[...]).astype(BF)

    @pl.when(is_first)
    def _():
        entering[...] = own_rows

    @pl.when(jnp.logical_not(is_first))
    def _():
        grad_out[...] = own_rows

    for tick in range(1, 9):
        for place in range(3):
            stage = tick - place
            if 1 <= stage <= 6:
                for number in order[3 * place : 3 * place + 3]:
                    gathers[number].step(stage)
    for number in order:
        gathers[number].finish()

    def cross(target, slot):
        return pltpu.make_async_remote_copy(
            src_ref=crossing,
            dst_ref=target,
            send_sem=cross_send.at[slot],
            recv_sem=cross_recv.at[slot],
            device_id={"section": 1 - section},
            device_id_type=MESH,
        )

    middle_copy = cross(entering, 0)
    grad_copy = cross(grad_out, 1)

    @pl.when(jnp.logical_not(is_first))
    def _():
        middle_copy.wait_recv()

    picks = jnp.where(
        lax.broadcasted_iota(jnp.int32, (PADDED, DP), 1) % PADDED == SHARD, 1.0, 0.0
    ).astype(BF)
    gains[0:1, :] = dot(picks, columns(whole, C_Q, DP))[0:1]
    gains[1:2, :] = dot(picks, columns(whole, C_G, DP))[0:1]
    matrix = entering[...].astype(F32)
    normed_one[...] = norm_forward(matrix, gains[0:1, :])

    cos_rows = jnp.concatenate([cosine[...]] * MICRO, axis=0)
    sin_rows = jnp.concatenate([sine[...]] * MICRO, axis=0)
    low_lane = lax.broadcasted_iota(jnp.int32, (ROWS, 128), 1) < HD

    for half in range(2):
        pre = dot(normed_one[...], columns(whole, C_Q + half * 512, 512))
        for tile in range(4):
            part = pre[:, tile * 128 : tile * 128 + 128]
            at = half * 512 + tile * 128
            queries[:, at : at + 128] = (part * cos_rows + swap_halves(part) * sin_rows).astype(BF)
    pre = dot(normed_one[...], columns(whole, C_KV, 640))
    for tile in range(5):
        part = pre[:, tile * 128 : tile * 128 + 128]
        if tile < 3:
            turned = part * cos_rows + swap_halves(part) * sin_rows
            part = turned if tile < 2 else jnp.where(low_lane, turned, part)
        key_value[:, tile * 128 : tile * 128 + 128] = part.astype(BF)

    def attend(seq, carry):
        rows = pl.ds(pl.multiple_of(seq * SEQ, SEQ), SEQ)
        query_pos = lax.broadcasted_iota(jnp.int32, (GROUP, SEQ, SEQ), 1).reshape(GROUP * SEQ, SEQ)
        key_pos = lax.broadcasted_iota(jnp.int32, (GROUP * SEQ, SEQ), 1)
        allowed = (key_pos <= query_pos) & (key_pos < lengths[seq, 0])
        query_rows = queries[rows, :]
        kv_rows = key_value[rows, :]
        heads = []
        for group in range(KV):
            at = group * GROUP * HD
            query = jnp.concatenate(
                [query_rows[:, at + h * HD : at + h * HD + HD] for h in range(GROUP)], axis=0
            )
            key = kv_rows[:, group * HD : group * HD + HD]
            value = kv_rows[:, (KV + group) * HD : (KV + group) * HD + HD]
            scores = jnp.where(allowed, dot_nt(query, key) * HD**-0.5, NEG)
            expos = jnp.exp(scores - jnp.max(scores, axis=1, keepdims=True))
            chances = expos / jnp.sum(expos, axis=1, keepdims=True)
            probs[seq, group] = chances
            out = dot(chances.astype(BF), value)
            heads.extend(out[h * SEQ : h * SEQ + SEQ] for h in range(GROUP))
        heads.append(jnp.zeros((SEQ, HD), F32))
        mixed[rows, :] = jnp.concatenate(heads, axis=1).astype(BF)
        return carry

    lax.fori_loop(0, MICRO, attend, 0)
    matrix = entering[...].astype(F32) + dot_nt(mixed[...], columns(whole, C_O, DP))
    resid[...] = matrix
    normed_two[...] = norm_forward(matrix, gains[1:2, :])
    total[...] = matrix

    def feed(step, carry):
        at = pl.multiple_of(step * CHUNK, CHUNK)
        here = pl.ds(at, CHUNK)
        gates = dot(normed_two[...], columns(whole, C_G + at, CHUNK))
        uppers = dot(normed_two[...], columns(whole, C_U + at, CHUNK))
        gate_up[:, here] = gates.astype(BF)
        gate_up[:, pl.ds(FF + at, CHUNK)] = uppers.astype(BF)
        hiddens = (gates / (1.0 + jnp.exp(-gates)) * uppers).astype(BF)
        hidden[:, here] = hiddens
        total[...] += dot_nt(hiddens, columns(whole, C_D + at, CHUNK))
        return carry

    lax.fori_loop(0, CHUNKS, feed, 0)

    def narrow(value):
        high = value.astype(BF)
        low = (value - high.astype(F32)).astype(BF)
        return dot_nt(high, spread[...]) + dot_nt(low, spread[...])

    @pl.when(is_first)
    def _():
        crossing[...] = total[...].astype(BF)
        middle_copy.start()
        middle_copy.wait_send()
        grad_copy.wait_recv()

    @pl.when(jnp.logical_not(is_first))
    def _():
        ends[...] = narrow(total[...])

    total[...] = jnp.zeros_like(total)

    def feed_back(step, carry):
        at = pl.multiple_of(step * CHUNK, CHUNK)
        here, beyond = pl.ds(at, CHUNK), pl.ds(FF + at, CHUNK)
        grad_hidden = dot(grad_out[...], columns(whole, C_D + at, CHUNK))
        gates = gate_up[:, here].astype(F32)
        opened = 1.0 / (1.0 + jnp.exp(-gates))
        grad_gate = (
            grad_hidden * gate_up[:, beyond].astype(F32) * (opened * (1.0 + gates * (1.0 - opened)))
        ).astype(BF)
        grad_up = (grad_hidden * (gates * opened)).astype(BF)
        gate_up[:, here] = grad_gate
        gate_up[:, beyond] = grad_up
        total[...] += dot_nt(grad_gate, columns(whole, C_G + at, CHUNK)) + dot_nt(
            grad_up, columns(whole, C_U + at, CHUNK)
        )
        return carry

    lax.fori_loop(0, CHUNKS, feed_back, 0)
    through, grad_gain = norm_backward(resid[...], gains[1:2, :], total[...])
    grad_gains[...] = jnp.zeros_like(grad_gains)
    grad_gains[1:2, 0:DP] = grad_gain
    through = through + grad_out[...].astype(F32)
    grad_resid[...] = through
    grad_branch[...] = through.astype(BF)
    grad_mixed[...] = dot(grad_branch[...], columns(whole, C_O, DP)).astype(BF)

    def attend_back(seq, carry):
        rows = pl.ds(pl.multiple_of(seq * SEQ, SEQ), SEQ)
        query_rows = queries[rows, :]
        kv_rows = key_value[rows, :]
        grad_rows = grad_mixed[rows, :]
        query_parts = []
        key_parts = []
        value_parts = []
        for group in range(KV):
            at = group * GROUP * HD
            query = jnp.concatenate(
                [query_rows[:, at + h * HD : at + h * HD + HD] for h in range(GROUP)], axis=0
            )
            grad = jnp.concatenate(
                [grad_rows[:, at + h * HD : at + h * HD + HD] for h in range(GROUP)], axis=0
            )
            key = kv_rows[:, group * HD : group * HD + HD]
            value = kv_rows[:, (KV + group) * HD : (KV + group) * HD + HD]
            chances = probs[seq, group]
            grad_probs = dot_nt(grad, value)
            inner = jnp.sum(chances * grad_probs, axis=1, keepdims=True)
            grad_scores = (chances * (grad_probs - inner)).astype(BF)
            grad_query = dot(grad_scores, key) * HD**-0.5
            query_parts.extend(grad_query[h * SEQ : h * SEQ + SEQ] for h in range(GROUP))
            key_parts.append(dot_tn(grad_scores, query) * HD**-0.5)
            value_parts.append(dot_tn(chances.astype(BF), grad))
        query_parts.append(jnp.zeros((SEQ, HD), F32))
        total[rows, :] = jnp.concatenate(query_parts, axis=1)
        grad_kv[rows, :] = jnp.concatenate(key_parts + value_parts, axis=1)
        return carry

    lax.fori_loop(0, MICRO, attend_back, 0)
    grad_query = grad_mixed
    for tile in range(8):
        part = total[:, tile * 128 : tile * 128 + 128]
        grad_query[:, tile * 128 : tile * 128 + 128] = (
            part * cos_rows - swap_halves(part) * sin_rows
        ).astype(BF)
    for tile in range(5):
        part = grad_kv[:, tile * 128 : tile * 128 + 128]
        if tile < 3:
            turned = part * cos_rows - swap_halves(part) * sin_rows
            part = turned if tile < 2 else jnp.where(low_lane, turned, part)
        key_value[:, tile * 128 : tile * 128 + 128] = part.astype(BF)
    grad_normed = dot_nt(grad_query[...], columns(whole, C_Q, DP)) + dot_nt(
        key_value[...], columns(whole, C_KV, 640)
    )
    through, grad_gain = norm_backward(entering[...].astype(F32), gains[0:1, :], grad_normed)
    grad_gains[0:1, 0:DP] = grad_gain
    through = through + grad_resid[...]

    @pl.when(is_first)
    def _():
        ends[...] = narrow(through)

    @pl.when(jnp.logical_not(is_first))
    def _():
        crossing[...] = through.astype(BF)
        grad_copy.start()
        grad_copy.wait_send()

    def put(left, right, first, count, gain):
        grad = dot_tn(left, right)
        if gain is not None:
            at, gain_row = gain
            row = lax.broadcasted_iota(jnp.int32, (DP, count), 0)
            column = lax.broadcasted_iota(jnp.int32, (DP, count), 1) + at
            own = (row % PADDED == SHARD) & (row // PADDED == column // PADDED)
            grad = jnp.where(own, gain_row, grad)
        whole[:, :, :, :, pl.ds(first, count)] = grad.astype(BF).reshape(4, 4, 4, PADDED, count)

    number_of = len(PIECES)
    scatters = [
        Scatter(
            number,
            whole,
            [lands[6 * number + 2 * phase : 6 * number + 2 * phase + 2] for phase in range(3)],
            scatter_send,
            scatter_recv,
            result,
            me,
            coords,
        )
        for number in range(number_of)
    ]

    def put_down(step, carry):
        at = pl.multiple_of(step * CHUNK, CHUNK)
        put(grad_out[...], hidden[:, pl.ds(at, CHUNK)], C_D + at, CHUNK, None)
        return carry

    lax.fori_loop(0, CHUNKS, put_down, 0)
    for number in (0, 1, 2):
        scatters[number].step(0)

    def put_gate_up(step, carry):
        at = pl.multiple_of(step * CHUNK, CHUNK)
        gain = (at, grad_gains[1:2, pl.ds(at, CHUNK)])
        put(normed_two[...], gate_up[:, pl.ds(at, CHUNK)], C_G + at, CHUNK, gain)
        return carry

    lax.fori_loop(0, 2 * CHUNKS, put_gate_up, 0)
    for number in (3, 4, 5):
        scatters[number].step(0)
    for half in range(2):
        at = half * CHUNK
        gain = (at, grad_gains[0:1, at : at + CHUNK])
        put(normed_one[...], grad_query[:, at : at + CHUNK], C_Q + at, CHUNK, gain)
        put(grad_branch[...], mixed[:, at : at + CHUNK], C_O + at, CHUNK, None)
    put(normed_one[...], key_value[...], C_KV, 640, None)
    for number in (6, 7, 8):
        scatters[number].step(0)

    for tick in range(1, 11):
        for place in range(3):
            stage = tick - place
            if 1 <= stage <= 8:
                for number in range(3 * place, 3 * place + 3):
                    scatters[number].step(stage)
    for number in range(number_of):
        scatters[number].finish()


def rope_tables():
    frequency = BASE ** (-(np.arange(HD // 2, dtype=np.float32) * np.float32(2.0 / HD)))
    angles = np.arange(SEQ, dtype=np.float32)[:, None] * frequency[None, :].astype(np.float32)
    cos, sin = np.cos(angles), np.sin(angles)
    return (
        np.concatenate([cos, cos, cos, cos], axis=1).astype(np.float32),
        np.concatenate([-sin, sin, -sin, sin], axis=1).astype(np.float32),
    )


def run_kernel(shard, rows_in, lengths, cosine, sine):
    scratch = [
        ((RING, RING, RING, PADDED, C_ALL), BF),
        ((ROWS, DP), BF),
        ((ROWS, DP), BF),
        ((ROWS, DP), BF),
        ((D, DP), BF),
        ((ROWS, DP), BF),
        ((ROWS, DP), BF),
        ((ROWS, 640), BF),
        ((MICRO, KV, GROUP * SEQ, SEQ), F32),
        ((ROWS, DP), BF),
        ((ROWS, DP), F32),
        ((ROWS, DP), BF),
        ((ROWS, 2 * FF), BF),
        ((ROWS, FF), BF),
        ((ROWS, DP), F32),
        ((ROWS, DP), F32),
        ((ROWS, DP), BF),
        ((ROWS, DP), BF),
        ((ROWS, 640), F32),
        ((8, DP), F32),
        ((8, 2 * FF), F32),
    ]
    scratch = [pltpu.VMEM(shape, kind) for shape, kind in scratch]
    count = len(PIECES)
    scratch += [
        pltpu.SemaphoreType.DMA((count, 12)),
        pltpu.SemaphoreType.DMA((count, 12)),
        pltpu.SemaphoreType.DMA((count, 18)),
        pltpu.SemaphoreType.DMA((count, 18)),
        pltpu.SemaphoreType.DMA((2,)),
        pltpu.SemaphoreType.DMA((2,)),
    ]
    for first, mid, last, _ in PIECES:
        for phase in range(3):
            for width in (mid - first, last - mid):
                shape = (3,) + (RING,) * (2 - phase) + (PADDED, width)
                scratch.append(pltpu.VMEM(shape, BF))
    vmem = pl.BlockSpec(memory_space=pltpu.VMEM)
    return pl.pallas_call(
        kernel,
        out_shape=(
            jax.ShapeDtypeStruct((ROWS, D), F32),
            jax.ShapeDtypeStruct((PADDED, C_ALL), F32),
        ),
        in_specs=[vmem, vmem, pl.BlockSpec(memory_space=pltpu.SMEM), vmem, vmem],
        out_specs=(vmem, vmem),
        scratch_shapes=scratch,
        compiler_params=pltpu.CompilerParams(
            collective_id=0, has_side_effects=True, vmem_limit_bytes=64 * 1024 * 1024
        ),
    )(shard, rows_in, lengths, cosine, sine)


def local(
    boundary, lengths, gain_attn, w_query, w_key, w_value, w_out, gain_mlp, w_gate, w_up, w_down
):
    me = lax.axis_index("dp")

    def pad(matrix, width):
        return jnp.pad(matrix, ((0, 0), (0, width - matrix.shape[1])))

    body = jnp.concatenate(
        [
            pad(w_query[0], 1024),
            pad(w_out[0].T, 1024),
            w_key[0],
            w_value[0],
            w_gate[0],
            w_up[0],
            w_down[0].T,
        ],
        axis=1,
    )
    ours = jnp.arange(DP // PADDED)[:, None] == me
    spread_one = jnp.where(ours, pad(gain_attn, PADDED), 0).reshape(1, DP)
    spread_two = jnp.where(ours, pad(gain_mlp, PADDED), 0).reshape(1, DP)
    last = jnp.concatenate(
        [
            spread_one,
            jnp.zeros((1, C_G - DP), BF),
            spread_two,
            jnp.zeros((1, C_ALL - C_G - DP), BF),
        ],
        axis=1,
    )
    shard = jnp.concatenate([body, last.astype(BF)], axis=0)
    cosine, sine = rope_tables()
    ends, result = run_kernel(
        shard,
        boundary[0].reshape(ROWS, D),
        lengths,
        jnp.asarray(cosine),
        jnp.asarray(sine),
    )
    body = result[:SHARD]

    def gain_of(first):
        return result[SHARD, first : first + DP].reshape(DP // PADDED, PADDED).sum(axis=0)[:SHARD]

    return (
        ends.reshape(1, MICRO, SEQ, D),
        gain_of(C_Q)[None],
        body[None, :, C_Q : C_Q + D],
        body[None, :, C_KV : C_KV + 320],
        body[None, :, C_KV + 320 : C_KV + 640],
        body[:, C_O : C_O + D].T[None],
        gain_of(C_G)[None],
        body[None, :, C_G : C_G + FF],
        body[None, :, C_U : C_U + FF],
        body[:, C_D : C_D + FF].T[None],
    )


def solution(mesh):
    row = P("section", "dp", None)
    column = P("section", None, "dp")
    gain = P("section", "dp")
    ends = P("section", None, "dp", None)
    weights = (gain, row, row, row, column, gain, row, row, column)
    return jax.shard_map(
        local,
        mesh=mesh,
        in_specs=(ends, P(None, "dp")) + weights,
        out_specs=(ends,) + weights,
        check_vma=False,
    )
```

```python
import numpy as np

import jax
import jax.numpy as jnp
from jax import lax
from jax.experimental import pallas as pl
from jax.experimental.pallas import tpu as pltpu
from jax.sharding import PartitionSpec as P

D = 960
DP = 1024
HQ = 15
KV = 5
GROUP = HQ // KV
HD = 64
FF = 2560
SEQ = 128
MICRO = 2
ROWS = MICRO * SEQ
RING = 4
SHARD = 15
PADDED = 16
EPS = 1e-05
NEG = -1e30
BASE = 10000.0
BF = jnp.bfloat16
F32 = jnp.float32
MESH = pl.DeviceIdType.MESH

C_Q = 0
C_O = 1024
C_KV = 2048
C_FF = 2688
CHUNKS = (1024, 1024, 512)
STARTS = (0, 1024, 2048)
SUB = 512
C_ALL = C_FF + 3 * FF

STRIDES = (16, 4, 1)
ORDERS = ((0, 1, 2), (1, 2, 0), (2, 0, 1))


def make_pieces():
    pieces = []
    for part in range(3):
        at = 896 * part
        pieces.append((at, at + (512 if part != 1 else 384), at + 896, ORDERS[part], at))
    at = C_FF
    for chunk, start in zip(CHUNKS, STARTS):
        for part in range(3):
            pieces.append((at, at + chunk // 2, at + chunk, ORDERS[part], C_FF + FF * part + start))
            at += chunk
    return pieces


PIECES = make_pieces()
GROUPS = len(CHUNKS) + 1


def position():
    me = lax.axis_index("dp")
    return me, (me // 16, (me // 4) % 4, me % 4)


def neighbour(me, coords, axis, step):
    here = coords[axis]
    return me + ((here + step) % RING - here) * STRIDES[axis]


def block(ref, order, phase, coords, at, first, last, later_full):
    index = [None, None, None]
    for place, axis in enumerate(order):
        if place == phase:
            index[axis] = at
        elif (place > phase) == later_full:
            index[axis] = slice(None)
        else:
            index[axis] = coords[axis]
    return ref.at[index[0], index[1], index[2], :, first:last]


def remote(src, dst, send, recv, device):
    return pltpu.make_async_remote_copy(
        src_ref=src,
        dst_ref=dst,
        send_sem=send,
        recv_sem=recv,
        device_id={"dp": device},
        device_id_type=MESH,
    )


class Gather:
    def __init__(self, number, whole, send, recv, me, coords):
        self.first, self.mid, self.last, self.order, _ = PIECES[number]
        self.whole, self.send, self.recv = whole, send.at[number], recv.at[number]
        self.me, self.coords = me, coords
        self.copies = []
        self.pending = []

    def go(self, phase, slot, at, first, last, step):
        axis = self.order[phase]
        view = block(self.whole, self.order, phase, self.coords, at, first, last, False)
        index = phase * 4 + slot
        copy = remote(
            view,
            view,
            self.send.at[index],
            self.recv.at[index],
            neighbour(self.me, self.coords, axis, step),
        )
        copy.start()
        self.copies.append(copy)
        return copy

    def step(self, number):
        phase, second = divmod(number, 2)
        for copy in self.pending:
            copy.wait_recv()
        self.pending = []
        if phase == 3:
            return
        here = self.coords[self.order[phase]]
        if not second:
            right = self.go(phase, 0, here, self.first, self.last, 1)
            left = self.go(phase, 1, here, self.first, self.last, -1)
        else:
            right = self.go(phase, 2, (here + 3) % RING, self.first, self.mid, 1)
            left = self.go(phase, 3, (here + 1) % RING, self.mid, self.last, -1)
        self.pending = [right, left]

    def finish(self):
        for copy in self.copies:
            copy.wait_send()


class Scatter:
    def __init__(self, number, whole, lands, send, recv, result, me, coords):
        self.first, self.mid, self.last, self.order, self.home = PIECES[number]
        self.whole, self.lands = whole, lands
        self.send, self.recv = send.at[number], recv.at[number]
        self.result = result
        self.me, self.coords = me, coords
        self.copies = []
        self.now = {}

    def view(self, phase, at, side):
        first, last = (self.first, self.mid) if side == 0 else (self.mid, self.last)
        return block(self.whole, self.order, phase, self.coords, at, first, last, True)

    def go(self, phase, slot, at, side, step):
        copy = remote(
            self.view(phase, at, side),
            self.lands[phase][side].at[slot],
            self.send.at[phase * 6 + side * 3 + slot],
            self.recv.at[phase * 6 + side * 3 + slot],
            neighbour(self.me, self.coords, self.order[phase], step),
        )
        copy.start()
        self.copies.append(copy)
        self.now[side, slot] = copy

    def add(self, phase, at, side, slots):
        view = self.view(phase, at, side)
        land = self.lands[phase][side]
        if phase == 2:
            total = view[...].astype(F32)
            for slot in slots:
                total = total + land[slot].astype(F32)
            if len(slots) == 2:
                first = self.home if side == 0 else self.home + self.mid - self.first
                for row in range(PADDED):
                    self.result[row, :, first : first + total.shape[1]] = total[row : row + 1]
            else:
                view[...] = total.astype(BF)
            return

        def one(step, carry):
            total = view[step].astype(F32)
            for slot in slots:
                total = total + land[slot, step].astype(F32)
            view[step] = total.astype(BF)
            return carry

        lax.fori_loop(0, RING, one, 0)

    def step(self, number):
        phase, part = divmod(number, 3)
        if phase == 3:
            return
        here = self.coords[self.order[phase]]
        ahead, across, behind = (here + 1) % RING, (here + 2) % RING, (here + 3) % RING
        if part == 0:
            self.go(phase, 0, across, 0, 1)
            self.go(phase, 0, across, 1, -1)
            self.go(phase, 1, ahead, 1, 1)
            self.go(phase, 1, behind, 0, -1)
        elif part == 1:
            self.now[0, 0].wait_recv()
            self.add(phase, ahead, 0, (0,))
            self.go(phase, 2, ahead, 0, 1)
            self.now[1, 0].wait_recv()
            self.add(phase, behind, 1, (0,))
            self.go(phase, 2, behind, 1, -1)
        else:
            for side in (0, 1):
                self.now[side, 1].wait_recv()
                self.now[side, 2].wait_recv()
                self.add(phase, here, side, (1, 2))

    def finish(self):
        for copy in self.copies:
            copy.wait_send()


def dot(left, right):
    return jnp.dot(left, right, preferred_element_type=F32)


def dot_nt(left, right):
    return lax.dot_general(left, right, (((1,), (1,)), ((), ())), preferred_element_type=F32)


def dot_tn(left, right):
    return lax.dot_general(left, right, (((0,), (0,)), ((), ())), preferred_element_type=F32)


def columns(whole, first, count):
    return whole[:, :, :, :, pl.ds(first, count)].reshape(DP, count)


def swap_halves(tile):
    lane = lax.broadcasted_iota(jnp.int32, tile.shape, 1)
    return jnp.where(lane % HD < HD // 2, pltpu.roll(tile, 96, 1), pltpu.roll(tile, 32, 1))


def norm_forward(matrix, gain):
    scale = lax.rsqrt(jnp.sum(matrix * matrix, axis=1, keepdims=True) * (1.0 / D) + EPS)
    return (matrix * scale * gain).astype(BF)


def norm_backward(matrix, gain, grad):
    scale = lax.rsqrt(jnp.sum(matrix * matrix, axis=1, keepdims=True) * (1.0 / D) + EPS)
    scaled = grad * gain
    inner = jnp.sum(scaled * matrix, axis=1, keepdims=True) * (1.0 / D)
    grad_matrix = scale * (scaled - matrix * (scale * scale * inner))
    grad_gain = jnp.sum(grad * matrix * scale, axis=0, keepdims=True)
    return grad_matrix, grad_gain


def kernel(
    w_query,
    w_out,
    w_key,
    w_value,
    w_gate,
    w_up,
    w_down,
    gain_attn,
    gain_mlp,
    rows_in,
    lengths,
    cosine,
    sine,
    ends,
    result,
    gain_result,
    whole,
    entering,
    grad_out,
    crossing,
    spread,
    normed_one,
    queries,
    key_value,
    probs,
    mixed,
    resid,
    normed_two,
    gate_up,
    hidden,
    total,
    total_back,
    grad_resid,
    grad_branch,
    grad_mixed,
    grad_kv,
    gains,
    grad_gains,
    gather_send,
    gather_recv,
    scatter_send,
    scatter_recv,
    cross_send,
    cross_recv,
    turn,
    *lands,
):
    section = lax.axis_index("section")
    me, coords = position()
    is_first = section == 0

    barrier = pltpu.get_barrier_semaphore()
    for axis in range(3):
        for step in (1, -1):
            pl.semaphore_signal(
                barrier,
                inc=1,
                device_id={"dp": neighbour(me, coords, axis, step)},
                device_id_type=MESH,
            )
    pl.semaphore_signal(barrier, inc=1, device_id={"section": 1 - section}, device_id_type=MESH)

    unit = jnp.where(
        lax.broadcasted_iota(jnp.int32, (PADDED, SHARD), 0)
        == lax.broadcasted_iota(jnp.int32, (PADDED, SHARD), 1),
        1.0,
        0.0,
    ).astype(BF)
    place = jnp.where(
        lax.broadcasted_iota(jnp.int32, (SHARD, DP), 1)
        == lax.broadcasted_iota(jnp.int32, (SHARD, DP), 0) + me * PADDED,
        1.0,
        0.0,
    ).astype(BF)
    last_row = lax.broadcasted_iota(jnp.int32, (PADDED, DP), 0) == SHARD

    def set_block(first, value):
        whole[coords[0], coords[1], coords[2], :, first : first + value.shape[1]] = value.astype(BF)

    def with_gain(weights, gain):
        body = jnp.concatenate(
            [dot(unit, weights[...]), jnp.zeros((PADDED, DP - D), F32)], axis=1
        )
        return jnp.where(last_row, dot(gain[...], place), body)

    set_block(C_Q, with_gain(w_query, gain_attn))
    set_block(C_O, with_gain(w_out, gain_mlp))
    set_block(C_KV, jnp.concatenate([dot(unit, w_key[...]), dot(unit, w_value[...])], axis=1))
    for index, (chunk, start) in enumerate(zip(CHUNKS, STARTS)):
        for part, weights in enumerate((w_gate, w_up, w_down)):
            set_block(
                C_FF + 3 * start + part * chunk, dot(unit, weights[:, start : start + chunk])
            )
    pl.semaphore_wait(barrier, 7)

    gathers = [
        Gather(number, whole, gather_send, gather_recv, me, coords)
        for number in range(len(PIECES))
    ]

    def gather(group, stage):
        for number in range(3 * group, 3 * group + 3):
            gathers[number].step(stage)

    for group in range(GROUPS):
        gather(group, 0)

    row = lax.broadcasted_iota(jnp.int32, (D, DP), 0)
    column = lax.broadcasted_iota(jnp.int32, (D, DP), 1)
    chosen = (column - column // PADDED == row) & (column % PADDED != SHARD)
    spread[...] = jnp.where(chosen, 1.0, 0.0).astype(BF)
    own_rows = jnp.concatenate(
        [dot_tn(rows_in[micro], spread[...]) for micro in range(MICRO)], axis=0
    ).astype(BF)

    @pl.when(is_first)
    def _():
        entering[...] = own_rows

    @pl.when(jnp.logical_not(is_first))
    def _():
        grad_out[...] = own_rows

    for group in range(GROUPS):
        gather(group, 1)

    @pl.when(jnp.logical_not(is_first))
    def _():
        pl.semaphore_wait(turn, 1)

    for stage in (2, 3):
        for group in range(GROUPS):
            gather(group, stage)
    gather(0, 4)
    gather(1, 4)
    gather(0, 5)
    gather(2, 4)
    gather(1, 5)
    gather(3, 4)

    @pl.when(is_first)
    def _():
        pl.semaphore_signal(turn, inc=1, device_id={"section": 1 - section}, device_id_type=MESH)

    gather(0, 6)

    def cross(target, slot):
        return pltpu.make_async_remote_copy(
            src_ref=crossing,
            dst_ref=target,
            send_sem=cross_send.at[slot],
            recv_sem=cross_recv.at[slot],
            device_id={"section": 1 - section},
            device_id_type=MESH,
        )

    middle_copy = cross(entering, 0)
    grad_copy = cross(grad_out, 1)

    picks = jnp.where(
        lax.broadcasted_iota(jnp.int32, (PADDED, DP), 1) % PADDED == SHARD, 1.0, 0.0
    ).astype(BF)
    gains[0:1, :] = dot(picks, columns(whole, C_Q, DP))[0:1]
    gains[1:2, :] = dot(picks, columns(whole, C_O, DP))[0:1]

    @pl.when(jnp.logical_not(is_first))
    def _():
        middle_copy.wait_recv()

    normed_one[...] = norm_forward(entering[...].astype(F32), gains[0:1, :])

    cos_rows = jnp.concatenate([cosine[...]] * MICRO, axis=0)
    sin_rows = jnp.concatenate([sine[...]] * MICRO, axis=0)
    low_lane = lax.broadcasted_iota(jnp.int32, (ROWS, 128), 1) < HD

    for half in range(2):
        pre = dot(normed_one[...], columns(whole, C_Q + half * 512, 512))
        for tile in range(4):
            part = pre[:, tile * 128 : tile * 128 + 128]
            at = half * 512 + tile * 128
            queries[:, at : at + 128] = (part * cos_rows + swap_halves(part) * sin_rows).astype(BF)
    pre = dot(normed_one[...], columns(whole, C_KV, 640))
    for tile in range(5):
        part = pre[:, tile * 128 : tile * 128 + 128]
        if tile < 3:
            turned = part * cos_rows + swap_halves(part) * sin_rows
            part = turned if tile < 2 else jnp.where(low_lane, turned, part)
        key_value[:, tile * 128 : tile * 128 + 128] = part.astype(BF)

    gather(2, 5)

    def attend(seq, carry):
        rows = pl.ds(pl.multiple_of(seq * SEQ, SEQ), SEQ)
        query_pos = lax.broadcasted_iota(jnp.int32, (GROUP, SEQ, SEQ), 1).reshape(GROUP * SEQ, SEQ)
        key_pos = lax.broadcasted_iota(jnp.int32, (GROUP * SEQ, SEQ), 1)
        allowed = (key_pos <= query_pos) & (key_pos < lengths[0, seq])
        query_rows = queries[rows, :]
        kv_rows = key_value[rows, :]
        heads = []
        for group in range(KV):
            at = group * GROUP * HD
            query = jnp.concatenate(
                [query_rows[:, at + h * HD : at + h * HD + HD] for h in range(GROUP)], axis=0
            )
            key = kv_rows[:, group * HD : group * HD + HD]
            value = kv_rows[:, (KV + group) * HD : (KV + group) * HD + HD]
            scores = jnp.where(allowed, dot_nt(query, key) * HD**-0.5, NEG)
            expos = jnp.exp(scores - jnp.max(scores, axis=1, keepdims=True))
            chances = expos / jnp.sum(expos, axis=1, keepdims=True)
            probs[seq, group] = chances
            out = dot(chances.astype(BF), value)
            heads.extend(out[h * SEQ : h * SEQ + SEQ] for h in range(GROUP))
        heads.append(jnp.zeros((SEQ, HD), F32))
        mixed[rows, :] = jnp.concatenate(heads, axis=1).astype(BF)
        return carry

    lax.fori_loop(0, MICRO, attend, 0)
    gather(3, 5)
    inside = lax.broadcasted_iota(jnp.int32, (ROWS, DP), 1) % PADDED != SHARD
    branch = jnp.where(inside, dot_nt(mixed[...], columns(whole, C_O, DP)), 0.0)
    matrix = entering[...].astype(F32) + branch
    resid[...] = matrix
    normed_two[...] = norm_forward(matrix, gains[1:2, :])
    total[...] = matrix

    def feed(chunk):
        base = C_FF + 3 * STARTS[chunk]
        width = CHUNKS[chunk]

        def one(step, carry):
            at = pl.multiple_of(step * SUB, SUB)
            unit_at = pl.multiple_of(STARTS[chunk] + at, SUB)
            gates = dot(normed_two[...], columns(whole, base + at, SUB))
            uppers = dot(normed_two[...], columns(whole, base + width + at, SUB))
            gate_up[:, pl.ds(unit_at, SUB)] = gates.astype(BF)
            gate_up[:, pl.ds(FF + unit_at, SUB)] = uppers.astype(BF)
            hiddens = (gates / (1.0 + jnp.exp(-gates)) * uppers).astype(BF)
            hidden[:, pl.ds(unit_at, SUB)] = hiddens
            total[...] += dot_nt(hiddens, columns(whole, base + 2 * width + at, SUB))
            return carry

        lax.fori_loop(0, width // SUB, one, 0)

    for chunk in range(len(CHUNKS)):
        gather(chunk + 1, 6)
        feed(chunk)

    def put_ends(value):
        high = value.astype(BF)
        low = (value - high.astype(F32)).astype(BF)
        for micro in range(MICRO):
            rows = slice(micro * SEQ, micro * SEQ + SEQ)
            ends[micro] = dot_nt(spread[...], high[rows]) + dot_nt(spread[...], low[rows])

    @pl.when(is_first)
    def _():
        crossing[...] = total[...].astype(BF)
        middle_copy.start()

    for piece in gathers:
        piece.finish()

    @pl.when(is_first)
    def _():
        middle_copy.wait_send()
        grad_copy.wait_recv()

    scatters = [
        Scatter(
            number,
            whole,
            [lands[6 * number + 2 * phase : 6 * number + 2 * phase + 2] for phase in range(3)],
            scatter_send,
            scatter_recv,
            result,
            me,
            coords,
        )
        for number in range(len(PIECES))
    ]
    parts_of = ((0,), (1,), (2, 3), (4,), (5, 6), (7,), (8,))

    def scatter(group, stage):
        for part in parts_of[stage]:
            for number in range(3 * group, 3 * group + 3):
                scatters[number].step(part)

    def put(left, right, first, count, gain=None):
        grad = dot_tn(left, right)
        if gain is not None:
            at, gain_row = gain
            row = lax.broadcasted_iota(jnp.int32, (DP, count), 0)
            column = lax.broadcasted_iota(jnp.int32, (DP, count), 1) + at
            own = (row % PADDED == SHARD) & (row // PADDED == column // PADDED)
            grad = jnp.where(own, gain_row, grad)
        whole[:, :, :, :, pl.ds(first, count)] = grad.astype(BF).reshape(4, 4, 4, PADDED, count)

    total_back[...] = jnp.zeros_like(total_back)

    def feed_back(chunk):
        base = C_FF + 3 * STARTS[chunk]
        width = CHUNKS[chunk]

        def one(step, carry):
            at = pl.multiple_of(step * SUB, SUB)
            unit_at = pl.multiple_of(STARTS[chunk] + at, SUB)
            grad_hidden = dot(grad_out[...], columns(whole, base + 2 * width + at, SUB))
            gates = gate_up[:, pl.ds(unit_at, SUB)].astype(F32)
            uppers = gate_up[:, pl.ds(FF + unit_at, SUB)].astype(F32)
            opened = 1.0 / (1.0 + jnp.exp(-gates))
            slope = opened * (1.0 + gates * (1.0 - opened))
            grad_gate = (grad_hidden * uppers * slope).astype(BF)
            grad_up = (grad_hidden * (gates * opened)).astype(BF)
            total_back[...] += dot_nt(grad_gate, columns(whole, base + at, SUB)) + dot_nt(
                grad_up, columns(whole, base + width + at, SUB)
            )
            put(normed_two[...], grad_gate, base + at, SUB)
            put(normed_two[...], grad_up, base + width + at, SUB)
            put(grad_out[...], hidden[:, pl.ds(unit_at, SUB)], base + 2 * width + at, SUB)
            return carry

        lax.fori_loop(0, width // SUB, one, 0)

    feed_back(2)
    scatter(3, 0)
    feed_back(1)
    scatter(2, 0)
    scatter(3, 1)
    feed_back(0)
    scatter(1, 0)
    scatter(3, 2)
    scatter(2, 1)

    through, grad_gain = norm_backward(resid[...], gains[1:2, :], total_back[...])
    grad_gains[1:2, :] = grad_gain
    through = through + grad_out[...].astype(F32)
    grad_resid[...] = through
    grad_branch[...] = through.astype(BF)
    grad_mixed[...] = dot(grad_branch[...], columns(whole, C_O, DP)).astype(BF)

    def attend_back(seq, carry):
        rows = pl.ds(pl.multiple_of(seq * SEQ, SEQ), SEQ)
        query_rows = queries[rows, :]
        kv_rows = key_value[rows, :]
        grad_rows = grad_mixed[rows, :]
        query_parts = []
        key_parts = []
        value_parts = []
        for group in range(KV):
            at = group * GROUP * HD
            query = jnp.concatenate(
                [query_rows[:, at + h * HD : at + h * HD + HD] for h in range(GROUP)], axis=0
            )
            grad = jnp.concatenate(
                [grad_rows[:, at + h * HD : at + h * HD + HD] for h in range(GROUP)], axis=0
            )
            key = kv_rows[:, group * HD : group * HD + HD]
            value = kv_rows[:, (KV + group) * HD : (KV + group) * HD + HD]
            chances = probs[seq, group]
            grad_probs = dot_nt(grad, value)
            inner = jnp.sum(chances * grad_probs, axis=1, keepdims=True)
            grad_scores = (chances * (grad_probs - inner)).astype(BF)
            grad_query = dot(grad_scores, key) * HD**-0.5
            query_parts.extend(grad_query[h * SEQ : h * SEQ + SEQ] for h in range(GROUP))
            key_parts.append(dot_tn(grad_scores, query) * HD**-0.5)
            value_parts.append(dot_tn(chances.astype(BF), grad))
        query_parts.append(jnp.zeros((SEQ, HD), F32))
        total_back[rows, :] = jnp.concatenate(query_parts, axis=1)
        grad_kv[rows, :] = jnp.concatenate(key_parts + value_parts, axis=1)
        return carry

    lax.fori_loop(0, MICRO, attend_back, 0)
    scatter(3, 3)
    scatter(2, 2)
    scatter(1, 1)
    grad_query = grad_mixed
    for tile in range(8):
        part = total_back[:, tile * 128 : tile * 128 + 128]
        grad_query[:, tile * 128 : tile * 128 + 128] = (
            part * cos_rows - swap_halves(part) * sin_rows
        ).astype(BF)
    for tile in range(5):
        part = grad_kv[:, tile * 128 : tile * 128 + 128]
        if tile < 3:
            turned = part * cos_rows - swap_halves(part) * sin_rows
            part = turned if tile < 2 else jnp.where(low_lane, turned, part)
        key_value[:, tile * 128 : tile * 128 + 128] = part.astype(BF)
    grad_normed = dot_nt(grad_query[...], columns(whole, C_Q, DP)) + dot_nt(
        key_value[...], columns(whole, C_KV, 640)
    )
    through, grad_gain = norm_backward(entering[...].astype(F32), gains[0:1, :], grad_normed)
    grad_gains[0:1, :] = grad_gain
    through = through + grad_resid[...]

    @pl.when(is_first)
    def _():
        total[...] = through

    @pl.when(jnp.logical_not(is_first))
    def _():
        crossing[...] = through.astype(BF)
        grad_copy.start()

    for half in range(2):
        at = half * SUB
        here = slice(at, at + SUB)
        put(normed_one[...], grad_query[:, here], C_Q + at, SUB, (at, grad_gains[0:1, here]))
        put(grad_branch[...], mixed[:, here], C_O + at, SUB, (at, grad_gains[1:2, here]))
    put(normed_one[...], key_value[...], C_KV, 640)
    scatter(0, 0)
    scatter(3, 4)
    scatter(2, 3)
    scatter(1, 2)
    put_ends(total[...])
    scatter(0, 1)
    scatter(3, 5)
    scatter(2, 4)
    scatter(1, 3)
    scatter(0, 2)
    scatter(3, 6)
    scatter(2, 5)
    scatter(1, 4)
    scatter(0, 3)
    scatter(2, 6)
    scatter(1, 5)
    scatter(0, 4)
    scatter(1, 6)
    scatter(0, 5)
    scatter(0, 6)
    for slot, first in enumerate((C_Q, C_O)):
        moved = pltpu.roll(result[SHARD, :, first : first + DP], DP - me * PADDED, 1)
        gain_result[slot : slot + 1, :] = moved[:, 0:128]

    @pl.when(jnp.logical_not(is_first))
    def _():
        grad_copy.wait_send()

    for piece in scatters:
        piece.finish()


def rope_tables():
    frequency = BASE ** (-(np.arange(HD // 2, dtype=np.float32) * np.float32(2.0 / HD)))
    angles = np.arange(SEQ, dtype=np.float32)[:, None] * frequency[None, :].astype(np.float32)
    cos, sin = np.cos(angles), np.sin(angles)
    return (
        np.concatenate([cos, cos, cos, cos], axis=1).astype(np.float32),
        np.concatenate([-sin, sin, -sin, sin], axis=1).astype(np.float32),
    )


def run_kernel(weights, gain_attn, gain_mlp, rows_in, lengths, cosine, sine):
    scratch = [
        ((RING, RING, RING, PADDED, C_ALL), BF),
        ((ROWS, DP), BF),
        ((ROWS, DP), BF),
        ((ROWS, DP), BF),
        ((D, DP), BF),
        ((ROWS, DP), BF),
        ((ROWS, DP), BF),
        ((ROWS, 640), BF),
        ((MICRO, KV, GROUP * SEQ, SEQ), F32),
        ((ROWS, DP), BF),
        ((ROWS, DP), F32),
        ((ROWS, DP), BF),
        ((ROWS, 2 * FF), BF),
        ((ROWS, FF), BF),
        ((ROWS, DP), F32),
        ((ROWS, DP), F32),
        ((ROWS, DP), F32),
        ((ROWS, DP), BF),
        ((ROWS, DP), BF),
        ((ROWS, 640), F32),
        ((8, DP), F32),
        ((8, DP), F32),
    ]
    scratch = [pltpu.VMEM(shape, kind) for shape, kind in scratch]
    count = len(PIECES)
    scratch += [
        pltpu.SemaphoreType.DMA((count, 12)),
        pltpu.SemaphoreType.DMA((count, 12)),
        pltpu.SemaphoreType.DMA((count, 18)),
        pltpu.SemaphoreType.DMA((count, 18)),
        pltpu.SemaphoreType.DMA((2,)),
        pltpu.SemaphoreType.DMA((2,)),
        pltpu.SemaphoreType.REGULAR,
    ]
    for first, mid, last, _, _ in PIECES:
        for phase in range(3):
            for width in (mid - first, last - mid):
                shape = (3,) + (RING,) * (2 - phase) + (PADDED, width)
                scratch.append(pltpu.VMEM(shape, BF))
    vmem = pl.BlockSpec(memory_space=pltpu.VMEM)
    return pl.pallas_call(
        kernel,
        out_shape=(
            jax.ShapeDtypeStruct((MICRO, D, SEQ), F32),
            jax.ShapeDtypeStruct((PADDED, 1, C_ALL), F32),
            jax.ShapeDtypeStruct((2, 128), F32),
        ),
        in_specs=[vmem] * 10 + [pl.BlockSpec(memory_space=pltpu.SMEM), vmem, vmem],
        out_specs=(vmem, vmem, vmem),
        scratch_shapes=scratch,
        compiler_params=pltpu.CompilerParams(
            collective_id=0, has_side_effects=True, vmem_limit_bytes=64 * 1024 * 1024
        ),
    )(*weights, gain_attn, gain_mlp, rows_in, lengths, cosine, sine)


def local(
    boundary, lengths, gain_attn, w_query, w_key, w_value, w_out, gain_mlp, w_gate, w_up, w_down
):
    cosine, sine = rope_tables()
    weights = (w_query[0], w_out[0].T, w_key[0], w_value[0], w_gate[0], w_up[0], w_down[0].T)
    ends, result, gains = run_kernel(
        weights,
        gain_attn,
        gain_mlp,
        boundary[0].transpose(0, 2, 1),
        lengths.T,
        jnp.asarray(cosine),
        jnp.asarray(sine),
    )

    def rows(first, count):
        return result[:SHARD, :, first : first + count].transpose(1, 0, 2)

    def turned(first, count):
        return result[:SHARD, :, first : first + count].transpose(1, 2, 0)

    return (
        ends.transpose(0, 2, 1)[None],
        gains[0:1, :SHARD],
        rows(C_Q, D),
        rows(C_KV, 320),
        rows(C_KV + 320, 320),
        turned(C_O, D),
        gains[1:2, :SHARD],
        rows(C_FF, FF),
        rows(C_FF + FF, FF),
        turned(C_FF + 2 * FF, FF),
    )


def solution(mesh):
    row = P("section", "dp", None)
    column = P("section", None, "dp")
    gain = P("section", "dp")
    ends = P("section", None, "dp", None)
    weights = (gain, row, row, row, column, gain, row, row, column)
    return jax.shard_map(
        local,
        mesh=mesh,
        in_specs=(ends, P(None, "dp")) + weights,
        out_specs=(ends,) + weights,
        check_vma=False,
    )
```

```python
import numpy as np

import jax
import jax.numpy as jnp
from jax import lax
from jax.experimental import pallas as pl
from jax.experimental.pallas import tpu as pltpu
from jax.sharding import PartitionSpec as P

D = 960
DP = 1024
HQ = 15
KV = 5
GROUP = HQ // KV
HD = 64
FF = 2560
SEQ = 128
MICRO = 2
ROWS = MICRO * SEQ
RING = 4
SHARD = 15
PADDED = 16
EPS = 1e-05
NEG = -1e30
BASE = 10000.0
BF = jnp.bfloat16
F32 = jnp.float32
MESH = pl.DeviceIdType.MESH

C_Q = 0
C_KV = 1024
C_O = 1664
C_FF = 2688
C_ALL = C_FF + 3 * FF
SUB = 512

STRIDES = (16, 4, 1)
ORDERS = ((0, 1, 2), (1, 2, 0), (2, 0, 1))

CHUNKS = ((0, 1024), (1024, 2048), (2048, 2560))
LARGE = [
    [(0, 512, 896, 0), (896, 1280, 1664, 1)],
    [(1664, 1792, 1792, 1), (1792, 2304, 2688, 2)],
] + [
    [
        (C_FF + FF * part + first, C_FF + FF * part + (first + last) // 2, C_FF + FF * part + last, part)
        for part in range(3)
    ]
    for first, last in CHUNKS
]
GROUPS = len(LARGE)
MERGED = [
    [(896 * part, 896 * part + 512, 896 * part + 896, part) for part in range(3)],
    [
        (C_FF + FF * part, C_FF + FF * part + FF // 2, C_FF + FF * part + FF, part)
        for part in range(3)
    ],
]


def position():
    me = lax.axis_index("dp")
    return me, (me // 16, (me // 4) % 4, me % 4)


def neighbour(me, coords, axis, step):
    here = coords[axis]
    return me + ((here + step) % RING - here) * STRIDES[axis]


def remote(src, dst, send, recv, device):
    return pltpu.make_async_remote_copy(
        src_ref=src,
        dst_ref=dst,
        send_sem=send,
        recv_sem=recv,
        device_id={"dp": device},
        device_id_type=MESH,
    )


class Ring:
    def __init__(self, piece, phase, later_full, whole, sems, me, coords):
        self.first, self.mid, self.last, part = piece
        self.order, self.phase, self.later_full = ORDERS[part], phase, later_full
        self.axis = self.order[phase]
        self.whole, self.sems = whole, sems
        self.me, self.coords = me, coords
        self.near = neighbour(me, coords, self.axis, 1)
        here = coords[self.axis]
        self.here, self.ahead, self.across, self.behind = [
            (here + step) % RING for step in range(4)
        ]

    def span(self, side):
        return ((self.first, self.last), (self.first, self.mid), (self.mid, self.last))[side]

    def view(self, at, side=0):
        first, last = self.span(side)
        index = [None, None, None]
        for place, axis in enumerate(self.order):
            if place == self.phase:
                index[axis] = at
            elif (place > self.phase) == self.later_full:
                index[axis] = slice(None)
            else:
                index[axis] = self.coords[axis]
        return self.whole.at[index[0], index[1], index[2], :, first:last]

    def widths(self):
        return [side for side in (1, 2) if self.span(side)[0] < self.span(side)[1]]

    def copy(self, src, dst, send, recv, step):
        remote(
            src,
            dst,
            self.sems.at[send],
            self.sems.at[recv],
            neighbour(self.me, self.coords, self.axis, step),
        ).start()

    def wait_recv(self, ref, sem):
        remote(ref, ref, self.sems.at[sem], self.sems.at[sem], self.near).wait_recv()

    def wait_send(self, ref, sem):
        remote(ref, ref, self.sems.at[sem], self.sems.at[sem], self.near).wait_send()


class DirectGather(Ring):
    count = 2

    def go(self):
        view = self.view(self.here)
        for step in (1, -1, 2):
            self.copy(view, view, 0, 1, step)

    def done(self):
        self.wait_recv(self.view(slice(0, 3)), 1)

    def finish(self):
        self.wait_send(self.view(slice(0, 3)), 0)


class RingGather(Ring):
    count = 3

    def go(self):
        view = self.view(self.here)
        self.copy(view, view, 0, 1, 1)
        self.copy(view, view, 0, 1, -1)

    def forward(self):
        self.wait_recv(self.view(slice(0, 2)), 1)
        sides = self.widths()
        right = self.view(self.behind, 1)
        self.copy(right, right, 0, 2, 1)
        if 2 in sides:
            left = self.view(self.ahead, 2)
            self.copy(left, left, 0, 2, -1)

    def done(self):
        self.wait_recv(self.view(self.here), 2)

    def finish(self):
        self.wait_send(self.view(slice(0, 3)), 0)


class DirectScatter(Ring):
    count = 2

    def __init__(self, *args, lands, result=None):
        super().__init__(*args)
        (self.land,), self.result = lands, result

    def go(self):
        for slot, step in enumerate((1, -1, 2)):
            at = (self.ahead, self.behind, self.across)[slot]
            self.copy(self.view(at), self.land.at[slot], 0, 1, step)

    def done(self):
        self.wait_recv(self.land, 1)
        view = self.view(self.here)
        if self.result is not None:
            total = view[...].astype(F32)
            for slot in range(3):
                total = total + self.land[slot].astype(F32)
            self.result(self.first, self.last, total)
            return

        def one(step, carry):
            total = view[step].astype(F32)
            for slot in range(3):
                total = total + self.land[slot, step].astype(F32)
            view[step] = total.astype(BF)
            return carry

        lax.fori_loop(0, RING, one, 0)

    def finish(self):
        self.wait_send(self.land, 0)


class RingScatter(Ring):
    count = 6

    def __init__(self, *args, lands):
        super().__init__(*args)
        self.lands = dict(zip(self.widths(), lands))

    def send(self, side, slot, at, step):
        base = 3 * (side - 1)
        self.copy(
            self.view(at, side), self.lands[side].at[slot], base, base + (1 if slot == 0 else 2), step
        )

    def add(self, at, side, slots):
        view, land = self.view(at, side), self.lands[side]

        def one(step, carry):
            total = view[step].astype(F32)
            for slot in slots:
                total = total + land[slot, step].astype(F32)
            view[step] = total.astype(BF)
            return carry

        lax.fori_loop(0, RING, one, 0)

    def go(self):
        sides = self.widths()
        self.send(1, 0, self.across, 1)
        if 2 in sides:
            self.send(2, 0, self.across, -1)
            self.send(2, 1, self.ahead, 1)
        self.send(1, 1, self.behind, -1)

    def forward(self):
        for side in self.widths():
            step, at = ((1, self.ahead), (-1, self.behind))[side - 1]
            self.wait_recv(self.lands[side].at[0], 3 * (side - 1) + 1)
            self.add(at, side, (0,))
            self.send(side, 2, at, step)

    def done(self):
        for side in self.widths():
            self.wait_recv(self.lands[side].at[1:3], 3 * (side - 1) + 2)
            self.add(self.here, side, (1, 2))

    def finish(self):
        for side in self.widths():
            self.wait_send(self.lands[side], 3 * (side - 1))


PLAN = {}
LANDS = []
SEMS = 0
for kind, cls, pieces, phase in (
    ("g1", DirectGather, MERGED, 0),
    ("g2", RingGather, MERGED, 1),
    ("g3", RingGather, LARGE, 2),
    ("s1", RingScatter, LARGE, 0),
    ("s2", DirectScatter, MERGED[:1], 1),
    ("s2", RingScatter, MERGED[1:], 1),
    ("s3", DirectScatter, MERGED, 2),
):
    for group in pieces:
        entries = []
        for piece in group:
            mine = []
            first, mid, last, _ = piece
            if cls is DirectScatter:
                mine = [last - first]
            elif cls is RingScatter:
                mine = [width for width in (mid - first, last - mid) if width]
            for width in mine:
                LANDS.append((3,) + (RING,) * (2 - phase) + (PADDED, width))
            entries.append((cls, piece, phase, SEMS, len(LANDS) - len(mine), len(LANDS)))
            SEMS += cls.count
        PLAN.setdefault(kind, []).append(entries)


def dot(left, right):
    return jnp.dot(left, right, preferred_element_type=F32)


def dot_nt(left, right):
    return lax.dot_general(left, right, (((1,), (1,)), ((), ())), preferred_element_type=F32)


def dot_tn(left, right):
    return lax.dot_general(left, right, (((0,), (0,)), ((), ())), preferred_element_type=F32)


def columns(whole, first, count):
    return whole[:, :, :, :, pl.ds(first, count)].reshape(DP, count)


def swap_halves(tile):
    lane = lax.broadcasted_iota(jnp.int32, tile.shape, 1)
    return jnp.where(lane % HD < HD // 2, pltpu.roll(tile, 96, 1), pltpu.roll(tile, 32, 1))


def norm_forward(matrix, gain):
    scale = lax.rsqrt(jnp.sum(matrix * matrix, axis=1, keepdims=True) * (1.0 / D) + EPS)
    return (matrix * scale * gain).astype(BF)


def norm_backward(matrix, gain, grad):
    scale = lax.rsqrt(jnp.sum(matrix * matrix, axis=1, keepdims=True) * (1.0 / D) + EPS)
    scaled = grad * gain
    inner = jnp.sum(scaled * matrix, axis=1, keepdims=True) * (1.0 / D)
    grad_matrix = scale * (scaled - matrix * (scale * scale * inner))
    grad_gain = jnp.sum(grad * matrix * scale, axis=0, keepdims=True)
    return grad_matrix, grad_gain


def kernel(
    w_query,
    w_out,
    w_key,
    w_value,
    w_gate,
    w_up,
    w_down,
    gain_attn,
    gain_mlp,
    rows_in,
    lengths,
    cosine,
    sine,
    ends,
    grad_w_query,
    grad_w_key,
    grad_w_value,
    grad_w_out,
    grad_w_gate,
    grad_w_up,
    grad_w_down,
    grad_gain_attn,
    grad_gain_mlp,
    whole,
    entering,
    grad_out,
    crossing,
    spread,
    normed_one,
    queries,
    key_value,
    probs,
    mixed,
    resid,
    normed_two,
    gate_up,
    hidden,
    total,
    total_back,
    grad_resid,
    grad_branch,
    grad_mixed,
    grad_kv,
    gains,
    grad_gains,
    sems,
    cross_send,
    cross_recv,
    turn,
    *lands,
):
    section = lax.axis_index("section")
    me, coords = position()
    is_first = section == 0

    barrier = pltpu.get_barrier_semaphore()
    for axis in range(3):
        for step in (1, -1, 2):
            pl.semaphore_signal(
                barrier,
                inc=1,
                device_id={"dp": neighbour(me, coords, axis, step)},
                device_id_type=MESH,
            )
    pl.semaphore_signal(barrier, inc=1, device_id={"section": 1 - section}, device_id_type=MESH)

    unit = jnp.where(
        lax.broadcasted_iota(jnp.int32, (PADDED, SHARD), 0)
        == lax.broadcasted_iota(jnp.int32, (PADDED, SHARD), 1),
        1.0,
        0.0,
    ).astype(BF)
    place = jnp.where(
        lax.broadcasted_iota(jnp.int32, (SHARD, DP), 1)
        == lax.broadcasted_iota(jnp.int32, (SHARD, DP), 0) + me * PADDED,
        1.0,
        0.0,
    ).astype(BF)
    last_row = lax.broadcasted_iota(jnp.int32, (PADDED, DP), 0) == SHARD

    def set_block(first, value):
        whole[coords[0], coords[1], coords[2], :, first : first + value.shape[1]] = value.astype(BF)

    def with_gain(weights, gain):
        body = jnp.concatenate(
            [dot(unit, weights[...]), jnp.zeros((PADDED, DP - D), F32)], axis=1
        )
        return jnp.where(last_row, dot(gain[...], place), body)

    set_block(C_Q, with_gain(w_query, gain_attn))
    set_block(C_O, with_gain(w_out, gain_mlp))
    set_block(C_KV, jnp.concatenate([dot(unit, w_key[...]), dot(unit, w_value[...])], axis=1))
    for part, weights in enumerate((w_gate, w_up, w_down)):
        set_block(C_FF + FF * part, dot(unit, weights[...]))
    pl.semaphore_wait(barrier, 10)

    homes = (
        (C_Q, D, grad_w_query),
        (C_KV, 320, grad_w_key),
        (C_KV + 320, 320, grad_w_value),
        (C_O, D, grad_w_out),
        (C_FF, FF, grad_w_gate),
        (C_FF + FF, FF, grad_w_up),
        (C_FF + 2 * FF, FF, grad_w_down),
    )

    def put_result(first, last, value):
        for start, count, ref in homes:
            low, high = max(first, start), min(last, start + count)
            if low < high:
                for row in range(SHARD):
                    ref[row, :, low - start : high - start] = value[
                        row : row + 1, low - first : high - first
                    ]
        for slot, start in enumerate((C_Q, C_O)):
            low, high = max(first, start), min(last, start + DP)
            if low < high:
                grad_gains[2 + slot : 3 + slot, low - start : high - start] = value[
                    SHARD : SHARD + 1, low - first : high - first
                ]

    started = []

    def make(entry):
        cls, piece, phase, sem, land, land_end = entry
        args = (piece, phase, cls in (RingScatter, DirectScatter), whole)
        args += (sems.at[sem : sem + cls.count], me, coords)
        if cls is DirectScatter:
            made = cls(
                *args, lands=lands[land:land_end], result=put_result if phase == 2 else None
            )
        elif cls is RingScatter:
            made = cls(*args, lands=lands[land:land_end])
        else:
            made = cls(*args)
        started.append(made)
        return made

    transfers = {
        kind: [[make(entry) for entry in group] for group in groups]
        for kind, groups in PLAN.items()
    }
    gathers = [made for made in started if isinstance(made, (DirectGather, RingGather))]
    scatters = [made for made in started if isinstance(made, (DirectScatter, RingScatter))]

    def run(kind, group, act):
        for made in transfers[kind][group]:
            getattr(made, act)()

    run("g1", 0, "go")
    run("g1", 1, "go")

    row = lax.broadcasted_iota(jnp.int32, (D, DP), 0)
    column = lax.broadcasted_iota(jnp.int32, (D, DP), 1)
    chosen = (column - column // PADDED == row) & (column % PADDED != SHARD)
    spread[...] = jnp.where(chosen, 1.0, 0.0).astype(BF)
    own_rows = jnp.concatenate(
        [dot_tn(rows_in[micro], spread[...]) for micro in range(MICRO)], axis=0
    ).astype(BF)

    @pl.when(is_first)
    def _():
        entering[...] = own_rows

    @pl.when(jnp.logical_not(is_first))
    def _():
        grad_out[...] = own_rows

    for group in range(2):
        run("g1", group, "done")
        run("g2", group, "go")

    def hand_over():
        @pl.when(is_first)
        def _():
            pl.semaphore_signal(
                turn, inc=1, device_id={"section": 1 - section}, device_id_type=MESH
            )

    def take_over():
        @pl.when(jnp.logical_not(is_first))
        def _():
            pl.semaphore_wait(turn, 1)

    for group in range(2):
        run("g2", group, "forward")
    run("g2", 0, "done")
    take_over()
    run("g3", 0, "go")
    run("g3", 1, "go")
    run("g2", 1, "done")
    run("g3", 2, "go")
    run("g3", 0, "forward")
    run("g3", 3, "go")
    run("g3", 1, "forward")
    run("g3", 4, "go")
    run("g3", 2, "forward")
    run("g3", 0, "done")

    def cross(target, slot):
        return pltpu.make_async_remote_copy(
            src_ref=crossing,
            dst_ref=target,
            send_sem=cross_send.at[slot],
            recv_sem=cross_recv.at[slot],
            device_id={"section": 1 - section},
            device_id_type=MESH,
        )

    middle_copy = cross(entering, 0)
    grad_copy = cross(grad_out, 1)

    picks = jnp.where(
        lax.broadcasted_iota(jnp.int32, (PADDED, DP), 1) % PADDED == SHARD, 1.0, 0.0
    ).astype(BF)
    gains[0:1, :] = dot(picks, columns(whole, C_Q, DP))[0:1]

    @pl.when(jnp.logical_not(is_first))
    def _():
        middle_copy.wait_recv()

    normed_one[...] = norm_forward(entering[...].astype(F32), gains[0:1, :])

    cos_rows = jnp.concatenate([cosine[...]] * MICRO, axis=0)
    sin_rows = jnp.concatenate([sine[...]] * MICRO, axis=0)
    low_lane = lax.broadcasted_iota(jnp.int32, (ROWS, 128), 1) < HD

    for half in range(2):
        pre = dot(normed_one[...], columns(whole, C_Q + half * 512, 512))
        for tile in range(4):
            part = pre[:, tile * 128 : tile * 128 + 128]
            at = half * 512 + tile * 128
            queries[:, at : at + 128] = (part * cos_rows + swap_halves(part) * sin_rows).astype(BF)
    pre = dot(normed_one[...], columns(whole, C_KV, 640))
    for tile in range(5):
        part = pre[:, tile * 128 : tile * 128 + 128]
        if tile < 3:
            turned = part * cos_rows + swap_halves(part) * sin_rows
            part = turned if tile < 2 else jnp.where(low_lane, turned, part)
        key_value[:, tile * 128 : tile * 128 + 128] = part.astype(BF)

    def attend(seq, carry):
        rows = pl.ds(pl.multiple_of(seq * SEQ, SEQ), SEQ)
        query_pos = lax.broadcasted_iota(jnp.int32, (GROUP, SEQ, SEQ), 1).reshape(GROUP * SEQ, SEQ)
        key_pos = lax.broadcasted_iota(jnp.int32, (GROUP * SEQ, SEQ), 1)
        allowed = (key_pos <= query_pos) & (key_pos < lengths[0, seq])
        query_rows = queries[rows, :]
        kv_rows = key_value[rows, :]
        heads = []
        for group in range(KV):
            at = group * GROUP * HD
            query = jnp.concatenate(
                [query_rows[:, at + h * HD : at + h * HD + HD] for h in range(GROUP)], axis=0
            )
            key = kv_rows[:, group * HD : group * HD + HD]
            value = kv_rows[:, (KV + group) * HD : (KV + group) * HD + HD]
            scores = jnp.where(allowed, dot_nt(query, key) * HD**-0.5, NEG)
            expos = jnp.exp(scores - jnp.max(scores, axis=1, keepdims=True))
            chances = expos / jnp.sum(expos, axis=1, keepdims=True)
            probs[seq, group] = chances
            out = dot(chances.astype(BF), value)
            heads.extend(out[h * SEQ : h * SEQ + SEQ] for h in range(GROUP))
        heads.append(jnp.zeros((SEQ, HD), F32))
        mixed[rows, :] = jnp.concatenate(heads, axis=1).astype(BF)
        return carry

    lax.fori_loop(0, MICRO, attend, 0)
    run("g3", 3, "forward")
    run("g3", 1, "done")
    gains[1:2, :] = dot(picks, columns(whole, C_O, DP))[0:1]
    inside = lax.broadcasted_iota(jnp.int32, (ROWS, DP), 1) % PADDED != SHARD
    branch = jnp.where(inside, dot_nt(mixed[...], columns(whole, C_O, DP)), 0.0)
    matrix = entering[...].astype(F32) + branch
    resid[...] = matrix
    normed_two[...] = norm_forward(matrix, gains[1:2, :])
    total[...] = matrix
    run("g3", 4, "forward")
    hand_over()

    def feed(chunk):
        def one(step, carry):
            unit_at = pl.multiple_of(step * SUB, SUB)
            gates = dot(normed_two[...], columns(whole, C_FF + unit_at, SUB))
            uppers = dot(normed_two[...], columns(whole, C_FF + FF + unit_at, SUB))
            gate_up[:, pl.ds(unit_at, SUB)] = gates.astype(BF)
            gate_up[:, pl.ds(FF + unit_at, SUB)] = uppers.astype(BF)
            hiddens = (gates / (1.0 + jnp.exp(-gates)) * uppers).astype(BF)
            hidden[:, pl.ds(unit_at, SUB)] = hiddens
            total[...] += dot_nt(hiddens, columns(whole, C_FF + 2 * FF + unit_at, SUB))
            return carry

        first, last = CHUNKS[chunk]
        lax.fori_loop(first // SUB, last // SUB, one, 0)

    for chunk in range(len(CHUNKS)):
        run("g3", chunk + 2, "done")
        feed(chunk)

    def put_ends(value):
        high = value.astype(BF)
        low = (value - high.astype(F32)).astype(BF)
        for micro in range(MICRO):
            rows = slice(micro * SEQ, micro * SEQ + SEQ)
            ends[micro] = dot_nt(spread[...], high[rows]) + dot_nt(spread[...], low[rows])

    @pl.when(is_first)
    def _():
        crossing[...] = total[...].astype(BF)
        middle_copy.start()

    for made in gathers:
        made.finish()

    @pl.when(is_first)
    def _():
        middle_copy.wait_send()
        grad_copy.wait_recv()

    def put(left, right, first, count, gain=None):
        grad = dot_tn(left, right)
        if gain is not None:
            at, gain_row = gain
            row = lax.broadcasted_iota(jnp.int32, (DP, count), 0)
            column = lax.broadcasted_iota(jnp.int32, (DP, count), 1) + at
            own = (row % PADDED == SHARD) & (row // PADDED == column // PADDED)
            grad = jnp.where(own, gain_row, grad)
        whole[:, :, :, :, pl.ds(first, count)] = grad.astype(BF).reshape(4, 4, 4, PADDED, count)

    total_back[...] = jnp.zeros_like(total_back)

    def feed_back(chunk):
        def one(step, carry):
            unit_at = pl.multiple_of(step * SUB, SUB)
            gate_at, up_at, down_at = [C_FF + FF * part + unit_at for part in range(3)]
            grad_hidden = dot(grad_out[...], columns(whole, down_at, SUB))
            gates = gate_up[:, pl.ds(unit_at, SUB)].astype(F32)
            uppers = gate_up[:, pl.ds(FF + unit_at, SUB)].astype(F32)
            opened = 1.0 / (1.0 + jnp.exp(-gates))
            slope = opened * (1.0 + gates * (1.0 - opened))
            grad_gate = (grad_hidden * uppers * slope).astype(BF)
            grad_up = (grad_hidden * (gates * opened)).astype(BF)
            total_back[...] += dot_nt(grad_gate, columns(whole, gate_at, SUB)) + dot_nt(
                grad_up, columns(whole, up_at, SUB)
            )
            put(normed_two[...], grad_gate, gate_at, SUB)
            put(normed_two[...], grad_up, up_at, SUB)
            put(grad_out[...], hidden[:, pl.ds(unit_at, SUB)], down_at, SUB)
            return carry

        first, last = CHUNKS[chunk]
        lax.fori_loop(first // SUB, last // SUB, one, 0)

    feed_back(2)
    run("s1", 4, "go")
    feed_back(1)
    run("s1", 3, "go")
    feed_back(0)
    run("s1", 2, "go")

    through, grad_gain = norm_backward(resid[...], gains[1:2, :], total_back[...])
    grad_gains[1:2, :] = grad_gain
    through = through + grad_out[...].astype(F32)
    grad_resid[...] = through
    grad_branch[...] = through.astype(BF)
    grad_mixed[...] = dot(grad_branch[...], columns(whole, C_O, DP)).astype(BF)
    for half in range(2):
        at = half * SUB
        here = slice(at, at + SUB)
        put(grad_branch[...], mixed[:, here], C_O + at, SUB, (at, grad_gains[1:2, here]))
    run("s1", 1, "go")
    run("s1", 4, "forward")

    def attend_back(seq, carry):
        rows = pl.ds(pl.multiple_of(seq * SEQ, SEQ), SEQ)
        query_rows = queries[rows, :]
        kv_rows = key_value[rows, :]
        grad_rows = grad_mixed[rows, :]
        query_parts = []
        key_parts = []
        value_parts = []
        for group in range(KV):
            at = group * GROUP * HD
            query = jnp.concatenate(
                [query_rows[:, at + h * HD : at + h * HD + HD] for h in range(GROUP)], axis=0
            )
            grad = jnp.concatenate(
                [grad_rows[:, at + h * HD : at + h * HD + HD] for h in range(GROUP)], axis=0
            )
            key = kv_rows[:, group * HD : group * HD + HD]
            value = kv_rows[:, (KV + group) * HD : (KV + group) * HD + HD]
            chances = probs[seq, group]
            grad_probs = dot_nt(grad, value)
            inner = jnp.sum(chances * grad_probs, axis=1, keepdims=True)
            grad_scores = (chances * (grad_probs - inner)).astype(BF)
            grad_query = dot(grad_scores, key) * HD**-0.5
            query_parts.extend(grad_query[h * SEQ : h * SEQ + SEQ] for h in range(GROUP))
            key_parts.append(dot_tn(grad_scores, query) * HD**-0.5)
            value_parts.append(dot_tn(chances.astype(BF), grad))
        query_parts.append(jnp.zeros((SEQ, HD), F32))
        total_back[rows, :] = jnp.concatenate(query_parts, axis=1)
        grad_kv[rows, :] = jnp.concatenate(key_parts + value_parts, axis=1)
        return carry

    lax.fori_loop(0, MICRO, attend_back, 0)
    run("s1", 3, "forward")
    grad_query = grad_mixed
    for tile in range(8):
        part = total_back[:, tile * 128 : tile * 128 + 128]
        grad_query[:, tile * 128 : tile * 128 + 128] = (
            part * cos_rows - swap_halves(part) * sin_rows
        ).astype(BF)
    for tile in range(5):
        part = grad_kv[:, tile * 128 : tile * 128 + 128]
        if tile < 3:
            turned = part * cos_rows - swap_halves(part) * sin_rows
            part = turned if tile < 2 else jnp.where(low_lane, turned, part)
        key_value[:, tile * 128 : tile * 128 + 128] = part.astype(BF)
    grad_normed = dot_nt(grad_query[...], columns(whole, C_Q, DP)) + dot_nt(
        key_value[...], columns(whole, C_KV, 640)
    )
    through, grad_gain = norm_backward(entering[...].astype(F32), gains[0:1, :], grad_normed)
    grad_gains[0:1, :] = grad_gain
    through = through + grad_resid[...]

    @pl.when(is_first)
    def _():
        total[...] = through

    @pl.when(jnp.logical_not(is_first))
    def _():
        crossing[...] = through.astype(BF)
        grad_copy.start()

    for half in range(2):
        at = half * SUB
        here = slice(at, at + SUB)
        put(normed_one[...], grad_query[:, here], C_Q + at, SUB, (at, grad_gains[0:1, here]))
    put(normed_one[...], key_value[...], C_KV, 640)
    run("s1", 0, "go")
    run("s1", 2, "forward")
    run("s1", 1, "forward")
    run("s1", 0, "forward")
    put_ends(total[...])
    for group in (4, 3, 2):
        run("s1", group, "done")
    run("s2", 1, "go")
    run("s1", 1, "done")
    run("s1", 0, "done")
    run("s2", 0, "go")
    run("s2", 1, "forward")
    run("s2", 0, "done")
    run("s3", 0, "go")
    run("s2", 1, "done")
    run("s3", 1, "go")
    run("s3", 0, "done")
    run("s3", 1, "done")
    for slot, gain_result in enumerate((grad_gain_attn, grad_gain_mlp)):
        moved = pltpu.roll(grad_gains[2 + slot : 3 + slot, :], DP - me * PADDED, 1)
        gain_result[...] = moved[:, 0:SHARD]

    @pl.when(jnp.logical_not(is_first))
    def _():
        grad_copy.wait_send()

    for made in scatters:
        made.finish()


def rope_tables():
    frequency = BASE ** (-(np.arange(HD // 2, dtype=np.float32) * np.float32(2.0 / HD)))
    angles = np.arange(SEQ, dtype=np.float32)[:, None] * frequency[None, :].astype(np.float32)
    cos, sin = np.cos(angles), np.sin(angles)
    return (
        np.concatenate([cos, cos, cos, cos], axis=1).astype(np.float32),
        np.concatenate([-sin, sin, -sin, sin], axis=1).astype(np.float32),
    )


def hand_on(*refs):
    count = len(refs) // 2
    for source, target in zip(refs[:count], refs[count:]):
        target[...] = source[...]


def run_kernel(weights, gain_attn, gain_mlp, rows_in, lengths, cosine, sine):
    scratch = [
        ((RING, RING, RING, PADDED, C_ALL), BF),
        ((ROWS, DP), BF),
        ((ROWS, DP), BF),
        ((ROWS, DP), BF),
        ((D, DP), BF),
        ((ROWS, DP), BF),
        ((ROWS, DP), BF),
        ((ROWS, 640), BF),
        ((MICRO, KV, GROUP * SEQ, SEQ), F32),
        ((ROWS, DP), BF),
        ((ROWS, DP), F32),
        ((ROWS, DP), BF),
        ((ROWS, 2 * FF), BF),
        ((ROWS, FF), BF),
        ((ROWS, DP), F32),
        ((ROWS, DP), F32),
        ((ROWS, DP), F32),
        ((ROWS, DP), BF),
        ((ROWS, DP), BF),
        ((ROWS, 640), F32),
        ((8, DP), F32),
        ((8, DP), F32),
    ]
    scratch = [pltpu.VMEM(shape, kind) for shape, kind in scratch]
    scratch += [
        pltpu.SemaphoreType.DMA((SEMS,)),
        pltpu.SemaphoreType.DMA((2,)),
        pltpu.SemaphoreType.DMA((2,)),
        pltpu.SemaphoreType.REGULAR,
    ]
    scratch += [pltpu.VMEM(shape, BF) for shape in LANDS]
    vmem = pl.BlockSpec(memory_space=pltpu.VMEM)
    made = pl.pallas_call(
        kernel,
        out_shape=(
            jax.ShapeDtypeStruct((MICRO, D, SEQ), F32),
            *(
                jax.ShapeDtypeStruct((SHARD, 1, width), F32)
                for width in (D, 320, 320, D, FF, FF, FF)
            ),
            jax.ShapeDtypeStruct((1, SHARD), F32),
            jax.ShapeDtypeStruct((1, SHARD), F32),
        ),
        in_specs=[vmem] * 10 + [pl.BlockSpec(memory_space=pltpu.SMEM), vmem, vmem],
        out_specs=(vmem,) * 10,
        scratch_shapes=scratch,
        compiler_params=pltpu.CompilerParams(
            collective_id=0, has_side_effects=True, vmem_limit_bytes=64 * 1024 * 1024
        ),
    )(*weights, gain_attn, gain_mlp, rows_in, lengths, cosine, sine)
    count = len(made)
    return pl.pallas_call(
        hand_on,
        out_shape=tuple(jax.ShapeDtypeStruct(one.shape, one.dtype) for one in made),
        in_specs=[vmem] * count,
        out_specs=(vmem,) * count,
    )(*made)


def local(
    boundary, lengths, gain_attn, w_query, w_key, w_value, w_out, gain_mlp, w_gate, w_up, w_down
):
    cosine, sine = rope_tables()
    weights = (w_query[0], w_out[0].T, w_key[0], w_value[0], w_gate[0], w_up[0], w_down[0].T)
    ends, query, key, value, out, gate, up, down, gain_one, gain_two = run_kernel(
        weights,
        gain_attn,
        gain_mlp,
        boundary[0].transpose(0, 2, 1),
        lengths.T,
        jnp.asarray(cosine),
        jnp.asarray(sine),
    )

    def rows(grad):
        return grad.transpose(1, 0, 2)

    def turned(grad):
        return grad.transpose(1, 2, 0)

    return (
        ends.transpose(0, 2, 1)[None],
        gain_one,
        rows(query),
        rows(key),
        rows(value),
        turned(out),
        gain_two,
        rows(gate),
        rows(up),
        turned(down),
    )


def solution(mesh):
    row = P("section", "dp", None)
    column = P("section", None, "dp")
    gain = P("section", "dp")
    ends = P("section", None, "dp", None)
    weights = (gain, row, row, row, column, gain, row, row, column)
    return jax.shard_map(
        local,
        mesh=mesh,
        in_specs=(ends, P(None, "dp")) + weights,
        out_specs=(ends,) + weights,
        check_vma=False,
    )
```

```python
import numpy as np

import jax
import jax.numpy as jnp
from jax import lax
from jax.experimental import pallas as pl
from jax.experimental.pallas import tpu as pltpu
from jax.sharding import PartitionSpec as P

D = 960
DP = 1024
HQ = 15
KV = 5
GROUP = HQ // KV
HD = 64
FF = 2560
SEQ = 128
MICRO = 2
ROWS = MICRO * SEQ
RING = 4
SHARD = 15
PADDED = 16
EPS = 1e-05
NEG = -1e30
BASE = 10000.0
BF = jnp.bfloat16
F32 = jnp.float32
MESH = pl.DeviceIdType.MESH

C_Q = 0
C_KV = 1024
C_O = 1664
C_FF = 2688
C_ALL = C_FF + 3 * FF
SUB = 512

STRIDES = (16, 4, 1)
ORDERS = ((0, 1, 2), (1, 2, 0), (2, 0, 1))

CHUNKS = ((0, 1024), (1024, 2048), (2048, 2560))
LARGE = [
    [(0, 512, 896, 0), (896, 1280, 1664, 1)],
    [(1664, 1792, 1792, 1), (1792, 2304, 2688, 2)],
] + [
    [
        (C_FF + FF * part + first, C_FF + FF * part + (first + last) // 2, C_FF + FF * part + last, part)
        for part in range(3)
    ]
    for first, last in CHUNKS
]
GROUPS = len(LARGE)
MERGED = [
    [(896 * part, 896 * part + 512, 896 * part + 896, part) for part in range(3)],
    [
        (C_FF + FF * part, C_FF + FF * part + FF // 2, C_FF + FF * part + FF, part)
        for part in range(3)
    ],
]


def position():
    me = lax.axis_index("dp")
    return me, (me // 16, (me // 4) % 4, me % 4)


def neighbour(me, coords, axis, step):
    here = coords[axis]
    return me + ((here + step) % RING - here) * STRIDES[axis]


def remote(src, dst, send, recv, device):
    return pltpu.make_async_remote_copy(
        src_ref=src,
        dst_ref=dst,
        send_sem=send,
        recv_sem=recv,
        device_id={"dp": device},
        device_id_type=MESH,
    )


class Ring:
    def __init__(self, piece, phase, later_full, whole, sems, me, coords):
        self.first, self.mid, self.last, part = piece
        self.order, self.phase, self.later_full = ORDERS[part], phase, later_full
        self.axis = self.order[phase]
        self.whole, self.sems = whole, sems
        self.me, self.coords = me, coords
        self.near = neighbour(me, coords, self.axis, 1)
        here = coords[self.axis]
        self.here, self.ahead, self.across, self.behind = [
            (here + step) % RING for step in range(4)
        ]

    def span(self, side):
        return ((self.first, self.last), (self.first, self.mid), (self.mid, self.last))[side]

    def view(self, at, side=0):
        first, last = self.span(side)
        index = [None, None, None]
        for place, axis in enumerate(self.order):
            if place == self.phase:
                index[axis] = at
            elif (place > self.phase) == self.later_full:
                index[axis] = slice(None)
            else:
                index[axis] = self.coords[axis]
        return self.whole.at[index[0], index[1], index[2], :, first:last]

    def widths(self):
        return [side for side in (1, 2) if self.span(side)[0] < self.span(side)[1]]

    def copy(self, src, dst, send, recv, step):
        remote(
            src,
            dst,
            self.sems.at[send],
            self.sems.at[recv],
            neighbour(self.me, self.coords, self.axis, step),
        ).start()

    def wait_recv(self, ref, sem):
        remote(ref, ref, self.sems.at[sem], self.sems.at[sem], self.near).wait_recv()

    def wait_send(self, ref, sem):
        remote(ref, ref, self.sems.at[sem], self.sems.at[sem], self.near).wait_send()


class DirectGather(Ring):
    count = 2

    def go(self):
        view = self.view(self.here)
        for step in (1, -1, 2):
            self.copy(view, view, 0, 1, step)

    def done(self):
        self.wait_recv(self.view(slice(0, 3)), 1)

    def finish(self):
        self.wait_send(self.view(slice(0, 3)), 0)


class RingGather(Ring):
    count = 3

    def go(self):
        view = self.view(self.here)
        self.copy(view, view, 0, 1, 1)
        self.copy(view, view, 0, 1, -1)

    def forward(self):
        self.wait_recv(self.view(slice(0, 2)), 1)
        sides = self.widths()
        right = self.view(self.behind, 1)
        self.copy(right, right, 0, 2, 1)
        if 2 in sides:
            left = self.view(self.ahead, 2)
            self.copy(left, left, 0, 2, -1)

    def done(self):
        self.wait_recv(self.view(self.here), 2)

    def finish(self):
        self.wait_send(self.view(slice(0, 3)), 0)


class DirectScatter(Ring):
    count = 2

    def __init__(self, *args, lands, result=None):
        super().__init__(*args)
        (self.land,), self.result = lands, result

    def go(self):
        for slot, step in enumerate((1, -1, 2)):
            at = (self.ahead, self.behind, self.across)[slot]
            self.copy(self.view(at), self.land.at[slot], 0, 1, step)

    def done(self):
        self.wait_recv(self.land, 1)
        view = self.view(self.here)
        if self.result is not None:
            total = view[...].astype(F32)
            for slot in range(3):
                total = total + self.land[slot].astype(F32)
            self.result(self.first, self.last, total)
            return

        def one(step, carry):
            total = view[step].astype(F32)
            for slot in range(3):
                total = total + self.land[slot, step].astype(F32)
            view[step] = total.astype(BF)
            return carry

        lax.fori_loop(0, RING, one, 0)

    def finish(self):
        self.wait_send(self.land, 0)


class RingScatter(Ring):
    count = 6

    def __init__(self, *args, lands):
        super().__init__(*args)
        self.lands = dict(zip(self.widths(), lands))

    def send(self, side, slot, at, step):
        base = 3 * (side - 1)
        self.copy(
            self.view(at, side), self.lands[side].at[slot], base, base + (1 if slot == 0 else 2), step
        )

    def add(self, at, side, slots):
        view, land = self.view(at, side), self.lands[side]

        def one(step, carry):
            total = view[step].astype(F32)
            for slot in slots:
                total = total + land[slot, step].astype(F32)
            view[step] = total.astype(BF)
            return carry

        lax.fori_loop(0, RING, one, 0)

    def go(self):
        sides = self.widths()
        self.send(1, 0, self.across, 1)
        if 2 in sides:
            self.send(2, 0, self.across, -1)
            self.send(2, 1, self.ahead, 1)
        self.send(1, 1, self.behind, -1)

    def forward(self):
        for side in self.widths():
            step, at = ((1, self.ahead), (-1, self.behind))[side - 1]
            self.wait_recv(self.lands[side].at[0], 3 * (side - 1) + 1)
            self.add(at, side, (0,))
            self.send(side, 2, at, step)

    def done(self):
        for side in self.widths():
            self.wait_recv(self.lands[side].at[1:3], 3 * (side - 1) + 2)
            self.add(self.here, side, (1, 2))

    def finish(self):
        for side in self.widths():
            self.wait_send(self.lands[side], 3 * (side - 1))


PLAN = {}
LANDS = []
SEMS = 0
for kind, cls, pieces, phase in (
    ("g1", DirectGather, MERGED, 0),
    ("g2", RingGather, MERGED, 1),
    ("g3", RingGather, LARGE, 2),
    ("s1", RingScatter, LARGE, 0),
    ("s2", DirectScatter, MERGED[:1], 1),
    ("s2", RingScatter, MERGED[1:], 1),
    ("s3", DirectScatter, MERGED, 2),
):
    for group in pieces:
        entries = []
        for piece in group:
            mine = []
            first, mid, last, _ = piece
            if cls is DirectScatter:
                mine = [last - first]
            elif cls is RingScatter:
                mine = [width for width in (mid - first, last - mid) if width]
            for width in mine:
                LANDS.append((3,) + (RING,) * (2 - phase) + (PADDED, width))
            entries.append((cls, piece, phase, SEMS, len(LANDS) - len(mine), len(LANDS)))
            SEMS += cls.count
        PLAN.setdefault(kind, []).append(entries)


def dot(left, right):
    return jnp.dot(left, right, preferred_element_type=F32)


def dot_nt(left, right):
    return lax.dot_general(left, right, (((1,), (1,)), ((), ())), preferred_element_type=F32)


def dot_tn(left, right):
    return lax.dot_general(left, right, (((0,), (0,)), ((), ())), preferred_element_type=F32)


def columns(whole, first, count):
    return whole[:, :, :, :, pl.ds(first, count)].reshape(DP, count)


def swap_halves(tile):
    lane = lax.broadcasted_iota(jnp.int32, tile.shape, 1)
    return jnp.where(lane % HD < HD // 2, pltpu.roll(tile, 96, 1), pltpu.roll(tile, 32, 1))


def norm_forward(matrix, gain):
    scale = lax.rsqrt(jnp.sum(matrix * matrix, axis=1, keepdims=True) * (1.0 / D) + EPS)
    return (matrix * scale * gain).astype(BF)


def norm_backward(matrix, gain, grad):
    scale = lax.rsqrt(jnp.sum(matrix * matrix, axis=1, keepdims=True) * (1.0 / D) + EPS)
    scaled = grad * gain
    inner = jnp.sum(scaled * matrix, axis=1, keepdims=True) * (1.0 / D)
    grad_matrix = scale * (scaled - matrix * (scale * scale * inner))
    grad_gain = jnp.sum(grad * matrix * scale, axis=0, keepdims=True)
    return grad_matrix, grad_gain


def kernel(
    w_query,
    w_out,
    w_key,
    w_value,
    w_gate,
    w_up,
    w_down,
    gain_attn,
    gain_mlp,
    rows_in,
    lengths,
    cosine,
    sine,
    ends,
    grad_w_query,
    grad_w_key,
    grad_w_value,
    grad_w_out,
    grad_w_gate,
    grad_w_up,
    grad_w_down,
    grad_gain_attn,
    grad_gain_mlp,
    whole,
    entering,
    grad_out,
    crossing,
    spread,
    normed_one,
    queries,
    key_value,
    probs,
    mixed,
    resid,
    normed_two,
    gate_up,
    hidden,
    total,
    total_back,
    grad_resid,
    grad_branch,
    grad_mixed,
    grad_kv,
    gains,
    grad_gains,
    sems,
    cross_send,
    cross_recv,
    turn,
    *lands,
):
    section = lax.axis_index("section")
    me, coords = position()
    is_first = section == 0

    barrier = pltpu.get_barrier_semaphore()
    for axis in range(3):
        for step in (1, -1, 2):
            pl.semaphore_signal(
                barrier,
                inc=1,
                device_id={"dp": neighbour(me, coords, axis, step)},
                device_id_type=MESH,
            )
    pl.semaphore_signal(barrier, inc=1, device_id={"section": 1 - section}, device_id_type=MESH)

    unit = jnp.where(
        lax.broadcasted_iota(jnp.int32, (PADDED, SHARD), 0)
        == lax.broadcasted_iota(jnp.int32, (PADDED, SHARD), 1),
        1.0,
        0.0,
    ).astype(BF)
    place = jnp.where(
        lax.broadcasted_iota(jnp.int32, (SHARD, DP), 1)
        == lax.broadcasted_iota(jnp.int32, (SHARD, DP), 0) + me * PADDED,
        1.0,
        0.0,
    ).astype(BF)
    last_row = lax.broadcasted_iota(jnp.int32, (PADDED, DP), 0) == SHARD

    def set_block(first, value):
        whole[coords[0], coords[1], coords[2], :, first : first + value.shape[1]] = value.astype(BF)

    def with_gain(weights, gain):
        body = jnp.concatenate(
            [dot(unit, weights[...]), jnp.zeros((PADDED, DP - D), F32)], axis=1
        )
        return jnp.where(last_row, dot(gain[...], place), body)

    set_block(C_Q, with_gain(w_query, gain_attn))
    set_block(C_O, with_gain(w_out, gain_mlp))
    set_block(C_KV, jnp.concatenate([dot(unit, w_key[...]), dot(unit, w_value[...])], axis=1))
    for part, weights in enumerate((w_gate, w_up, w_down)):
        set_block(C_FF + FF * part, dot(unit, weights[...]))
    pl.semaphore_wait(barrier, 10)

    homes = (
        (C_Q, D, grad_w_query),
        (C_KV, 320, grad_w_key),
        (C_KV + 320, 320, grad_w_value),
        (C_O, D, grad_w_out),
        (C_FF, FF, grad_w_gate),
        (C_FF + FF, FF, grad_w_up),
        (C_FF + 2 * FF, FF, grad_w_down),
    )

    def put_result(first, last, value):
        for start, count, ref in homes:
            low, high = max(first, start), min(last, start + count)
            if low < high:
                for row in range(SHARD):
                    ref[row, :, low - start : high - start] = value[
                        row : row + 1, low - first : high - first
                    ]
        for slot, start in enumerate((C_Q, C_O)):
            low, high = max(first, start), min(last, start + DP)
            if low < high:
                grad_gains[2 + slot : 3 + slot, low - start : high - start] = value[
                    SHARD : SHARD + 1, low - first : high - first
                ]

    started = []

    def make(entry):
        cls, piece, phase, sem, land, land_end = entry
        args = (piece, phase, cls in (RingScatter, DirectScatter), whole)
        args += (sems.at[sem : sem + cls.count], me, coords)
        if cls is DirectScatter:
            made = cls(
                *args, lands=lands[land:land_end], result=put_result if phase == 2 else None
            )
        elif cls is RingScatter:
            made = cls(*args, lands=lands[land:land_end])
        else:
            made = cls(*args)
        started.append(made)
        return made

    transfers = {
        kind: [[make(entry) for entry in group] for group in groups]
        for kind, groups in PLAN.items()
    }
    scatters = [made for made in started if isinstance(made, (DirectScatter, RingScatter))]

    def run(kind, group, act):
        for made in transfers[kind][group]:
            getattr(made, act)()

    run("g1", 0, "go")
    run("g1", 1, "go")

    row = lax.broadcasted_iota(jnp.int32, (D, DP), 0)
    column = lax.broadcasted_iota(jnp.int32, (D, DP), 1)
    chosen = (column - column // PADDED == row) & (column % PADDED != SHARD)
    spread[...] = jnp.where(chosen, 1.0, 0.0).astype(BF)
    own_rows = jnp.concatenate(
        [dot_tn(rows_in[micro], spread[...]) for micro in range(MICRO)], axis=0
    ).astype(BF)

    @pl.when(is_first)
    def _():
        entering[...] = own_rows

    @pl.when(jnp.logical_not(is_first))
    def _():
        grad_out[...] = own_rows

    for group in range(2):
        run("g1", group, "done")
        run("g2", group, "go")

    def hand_over():
        @pl.when(is_first)
        def _():
            pl.semaphore_signal(
                turn, inc=1, device_id={"section": 1 - section}, device_id_type=MESH
            )

    def take_over():
        @pl.when(jnp.logical_not(is_first))
        def _():
            pl.semaphore_wait(turn, 1)

    for group in range(2):
        run("g2", group, "forward")
    run("g2", 0, "done")
    take_over()
    run("g3", 0, "go")
    run("g3", 1, "go")
    run("g2", 1, "done")
    run("g3", 2, "go")
    run("g3", 0, "forward")
    run("g3", 3, "go")
    run("g3", 1, "forward")
    run("g3", 4, "go")
    run("g3", 2, "forward")
    run("g3", 0, "done")

    def cross(target, slot):
        return pltpu.make_async_remote_copy(
            src_ref=crossing,
            dst_ref=target,
            send_sem=cross_send.at[slot],
            recv_sem=cross_recv.at[slot],
            device_id={"section": 1 - section},
            device_id_type=MESH,
        )

    middle_copy = cross(entering, 0)
    grad_copy = cross(grad_out, 1)

    picks = jnp.where(
        lax.broadcasted_iota(jnp.int32, (PADDED, DP), 1) % PADDED == SHARD, 1.0, 0.0
    ).astype(BF)
    gains[0:1, :] = dot(picks, columns(whole, C_Q, DP))[0:1]

    @pl.when(jnp.logical_not(is_first))
    def _():
        middle_copy.wait_recv()

    normed_one[...] = norm_forward(entering[...].astype(F32), gains[0:1, :])

    cos_rows = jnp.concatenate([cosine[...]] * MICRO, axis=0)
    sin_rows = jnp.concatenate([sine[...]] * MICRO, axis=0)
    low_lane = lax.broadcasted_iota(jnp.int32, (ROWS, 128), 1) < HD

    for half in range(2):
        pre = dot(normed_one[...], columns(whole, C_Q + half * 512, 512))
        for tile in range(4):
            part = pre[:, tile * 128 : tile * 128 + 128]
            at = half * 512 + tile * 128
            queries[:, at : at + 128] = (part * cos_rows + swap_halves(part) * sin_rows).astype(BF)
    pre = dot(normed_one[...], columns(whole, C_KV, 640))
    for tile in range(5):
        part = pre[:, tile * 128 : tile * 128 + 128]
        if tile < 3:
            turned = part * cos_rows + swap_halves(part) * sin_rows
            part = turned if tile < 2 else jnp.where(low_lane, turned, part)
        key_value[:, tile * 128 : tile * 128 + 128] = part.astype(BF)

    def attend(seq, carry):
        rows = pl.ds(pl.multiple_of(seq * SEQ, SEQ), SEQ)
        query_pos = lax.broadcasted_iota(jnp.int32, (GROUP, SEQ, SEQ), 1).reshape(GROUP * SEQ, SEQ)
        key_pos = lax.broadcasted_iota(jnp.int32, (GROUP * SEQ, SEQ), 1)
        allowed = (key_pos <= query_pos) & (key_pos < lengths[0, seq])
        query_rows = queries[rows, :]
        kv_rows = key_value[rows, :]
        heads = []
        for group in range(KV):
            at = group * GROUP * HD
            query = jnp.concatenate(
                [query_rows[:, at + h * HD : at + h * HD + HD] for h in range(GROUP)], axis=0
            )
            key = kv_rows[:, group * HD : group * HD + HD]
            value = kv_rows[:, (KV + group) * HD : (KV + group) * HD + HD]
            scores = jnp.where(allowed, dot_nt(query, key) * HD**-0.5, NEG)
            expos = jnp.exp(scores - jnp.max(scores, axis=1, keepdims=True))
            chances = expos / jnp.sum(expos, axis=1, keepdims=True)
            probs[seq, group] = chances
            out = dot(chances.astype(BF), value)
            heads.extend(out[h * SEQ : h * SEQ + SEQ] for h in range(GROUP))
        heads.append(jnp.zeros((SEQ, HD), F32))
        mixed[rows, :] = jnp.concatenate(heads, axis=1).astype(BF)
        return carry

    lax.fori_loop(0, MICRO, attend, 0)
    run("g3", 3, "forward")
    run("g3", 1, "done")
    gains[1:2, :] = dot(picks, columns(whole, C_O, DP))[0:1]
    inside = lax.broadcasted_iota(jnp.int32, (ROWS, DP), 1) % PADDED != SHARD
    branch = jnp.where(inside, dot_nt(mixed[...], columns(whole, C_O, DP)), 0.0)
    matrix = entering[...].astype(F32) + branch
    resid[...] = matrix
    normed_two[...] = norm_forward(matrix, gains[1:2, :])
    total[...] = matrix
    run("g3", 4, "forward")
    hand_over()

    def feed(chunk):
        def one(step, carry):
            unit_at = pl.multiple_of(step * SUB, SUB)
            gates = dot(normed_two[...], columns(whole, C_FF + unit_at, SUB))
            uppers = dot(normed_two[...], columns(whole, C_FF + FF + unit_at, SUB))
            gate_up[:, pl.ds(unit_at, SUB)] = gates.astype(BF)
            gate_up[:, pl.ds(FF + unit_at, SUB)] = uppers.astype(BF)
            hiddens = (gates / (1.0 + jnp.exp(-gates)) * uppers).astype(BF)
            hidden[:, pl.ds(unit_at, SUB)] = hiddens
            total[...] += dot_nt(hiddens, columns(whole, C_FF + 2 * FF + unit_at, SUB))
            return carry

        first, last = CHUNKS[chunk]
        lax.fori_loop(first // SUB, last // SUB, one, 0)

    def put(left, right, first, count, gain=None):
        grad = dot_tn(left, right)
        if gain is not None:
            at, gain_row = gain
            row = lax.broadcasted_iota(jnp.int32, (DP, count), 0)
            column = lax.broadcasted_iota(jnp.int32, (DP, count), 1) + at
            own = (row % PADDED == SHARD) & (row // PADDED == column // PADDED)
            grad = jnp.where(own, gain_row, grad)
        whole[:, :, :, :, pl.ds(first, count)] = grad.astype(BF).reshape(4, 4, 4, PADDED, count)

    def feed_back(chunk):
        def one(step, carry):
            unit_at = pl.multiple_of(step * SUB, SUB)
            gate_at, up_at, down_at = [C_FF + FF * part + unit_at for part in range(3)]
            grad_hidden = dot(grad_out[...], columns(whole, down_at, SUB))
            gates = gate_up[:, pl.ds(unit_at, SUB)].astype(F32)
            uppers = gate_up[:, pl.ds(FF + unit_at, SUB)].astype(F32)
            opened = 1.0 / (1.0 + jnp.exp(-gates))
            slope = opened * (1.0 + gates * (1.0 - opened))
            grad_gate = (grad_hidden * uppers * slope).astype(BF)
            grad_up = (grad_hidden * (gates * opened)).astype(BF)
            total_back[...] += dot_nt(grad_gate, columns(whole, gate_at, SUB)) + dot_nt(
                grad_up, columns(whole, up_at, SUB)
            )
            put(normed_two[...], grad_gate, gate_at, SUB)
            put(normed_two[...], grad_up, up_at, SUB)
            put(grad_out[...], hidden[:, pl.ds(unit_at, SUB)], down_at, SUB)
            return carry

        first, last = CHUNKS[chunk]
        lax.fori_loop(first // SUB, last // SUB, one, 0)

    def turn_back(chunk):
        feed_back(chunk)
        run("s1", chunk + 2, "go")

    total_back[...] = jnp.zeros_like(total_back)
    run("g1", 1, "finish")
    run("g2", 1, "finish")
    for chunk in range(len(CHUNKS)):
        run("g3", chunk + 2, "done")
        run("g3", chunk + 2, "finish")
        feed(chunk)

        @pl.when(jnp.logical_not(is_first))
        def _():
            turn_back(chunk)


    def put_ends(value):
        high = value.astype(BF)
        low = (value - high.astype(F32)).astype(BF)
        for micro in range(MICRO):
            rows = slice(micro * SEQ, micro * SEQ + SEQ)
            ends[micro] = dot_nt(spread[...], high[rows]) + dot_nt(spread[...], low[rows])

    @pl.when(is_first)
    def _():
        crossing[...] = total[...].astype(BF)
        middle_copy.start()

    for kind, group in (("g1", 0), ("g2", 0), ("g3", 0), ("g3", 1)):
        run(kind, group, "finish")

    @pl.when(is_first)
    def _():
        middle_copy.wait_send()
        grad_copy.wait_recv()

    @pl.when(is_first)
    def _():
        for chunk in range(len(CHUNKS)):
            turn_back(chunk)

    through, grad_gain = norm_backward(resid[...], gains[1:2, :], total_back[...])
    grad_gains[1:2, :] = grad_gain
    through = through + grad_out[...].astype(F32)
    grad_resid[...] = through
    grad_branch[...] = through.astype(BF)
    grad_mixed[...] = dot(grad_branch[...], columns(whole, C_O, DP)).astype(BF)
    for half in range(2):
        at = half * SUB
        here = slice(at, at + SUB)
        put(grad_branch[...], mixed[:, here], C_O + at, SUB, (at, grad_gains[1:2, here]))
    run("s1", 1, "go")
    run("s1", 2, "forward")

    def attend_back(seq, carry):
        rows = pl.ds(pl.multiple_of(seq * SEQ, SEQ), SEQ)
        query_rows = queries[rows, :]
        kv_rows = key_value[rows, :]
        grad_rows = grad_mixed[rows, :]
        query_parts = []
        key_parts = []
        value_parts = []
        for group in range(KV):
            at = group * GROUP * HD
            query = jnp.concatenate(
                [query_rows[:, at + h * HD : at + h * HD + HD] for h in range(GROUP)], axis=0
            )
            grad = jnp.concatenate(
                [grad_rows[:, at + h * HD : at + h * HD + HD] for h in range(GROUP)], axis=0
            )
            key = kv_rows[:, group * HD : group * HD + HD]
            value = kv_rows[:, (KV + group) * HD : (KV + group) * HD + HD]
            chances = probs[seq, group]
            grad_probs = dot_nt(grad, value)
            inner = jnp.sum(chances * grad_probs, axis=1, keepdims=True)
            grad_scores = (chances * (grad_probs - inner)).astype(BF)
            grad_query = dot(grad_scores, key) * HD**-0.5
            query_parts.extend(grad_query[h * SEQ : h * SEQ + SEQ] for h in range(GROUP))
            key_parts.append(dot_tn(grad_scores, query) * HD**-0.5)
            value_parts.append(dot_tn(chances.astype(BF), grad))
        query_parts.append(jnp.zeros((SEQ, HD), F32))
        total_back[rows, :] = jnp.concatenate(query_parts, axis=1)
        grad_kv[rows, :] = jnp.concatenate(key_parts + value_parts, axis=1)
        return carry

    lax.fori_loop(0, MICRO, attend_back, 0)
    run("s1", 3, "forward")
    grad_query = grad_mixed
    for tile in range(8):
        part = total_back[:, tile * 128 : tile * 128 + 128]
        grad_query[:, tile * 128 : tile * 128 + 128] = (
            part * cos_rows - swap_halves(part) * sin_rows
        ).astype(BF)
    for tile in range(5):
        part = grad_kv[:, tile * 128 : tile * 128 + 128]
        if tile < 3:
            turned = part * cos_rows - swap_halves(part) * sin_rows
            part = turned if tile < 2 else jnp.where(low_lane, turned, part)
        key_value[:, tile * 128 : tile * 128 + 128] = part.astype(BF)
    grad_normed = dot_nt(grad_query[...], columns(whole, C_Q, DP)) + dot_nt(
        key_value[...], columns(whole, C_KV, 640)
    )
    through, grad_gain = norm_backward(entering[...].astype(F32), gains[0:1, :], grad_normed)
    grad_gains[0:1, :] = grad_gain
    through = through + grad_resid[...]

    @pl.when(is_first)
    def _():
        total[...] = through

    @pl.when(jnp.logical_not(is_first))
    def _():
        crossing[...] = through.astype(BF)
        grad_copy.start()

    for half in range(2):
        at = half * SUB
        here = slice(at, at + SUB)
        put(normed_one[...], grad_query[:, here], C_Q + at, SUB, (at, grad_gains[0:1, here]))
    put(normed_one[...], key_value[...], C_KV, 640)
    run("s1", 0, "go")
    run("s1", 4, "forward")
    run("s1", 1, "forward")
    run("s1", 0, "forward")
    put_ends(total[...])
    for group in (2, 3, 4):
        run("s1", group, "done")
    run("s2", 1, "go")
    run("s1", 1, "done")
    run("s1", 0, "done")
    run("s2", 0, "go")
    run("s2", 1, "forward")
    run("s2", 0, "done")
    run("s3", 0, "go")
    run("s2", 1, "done")
    run("s3", 1, "go")
    run("s3", 0, "done")
    run("s3", 1, "done")
    for slot, gain_result in enumerate((grad_gain_attn, grad_gain_mlp)):
        moved = pltpu.roll(grad_gains[2 + slot : 3 + slot, :], DP - me * PADDED, 1)
        gain_result[...] = moved[:, 0:SHARD]

    @pl.when(jnp.logical_not(is_first))
    def _():
        grad_copy.wait_send()

    for made in scatters:
        made.finish()


def rope_tables():
    frequency = BASE ** (-(np.arange(HD // 2, dtype=np.float32) * np.float32(2.0 / HD)))
    angles = np.arange(SEQ, dtype=np.float32)[:, None] * frequency[None, :].astype(np.float32)
    cos, sin = np.cos(angles), np.sin(angles)
    return (
        np.concatenate([cos, cos, cos, cos], axis=1).astype(np.float32),
        np.concatenate([-sin, sin, -sin, sin], axis=1).astype(np.float32),
    )


def hand_on(*refs):
    count = len(refs) // 2
    for source, target in zip(refs[:count], refs[count:]):
        target[...] = source[...]


def run_kernel(weights, gain_attn, gain_mlp, rows_in, lengths, cosine, sine):
    scratch = [
        ((RING, RING, RING, PADDED, C_ALL), BF),
        ((ROWS, DP), BF),
        ((ROWS, DP), BF),
        ((ROWS, DP), BF),
        ((D, DP), BF),
        ((ROWS, DP), BF),
        ((ROWS, DP), BF),
        ((ROWS, 640), BF),
        ((MICRO, KV, GROUP * SEQ, SEQ), F32),
        ((ROWS, DP), BF),
        ((ROWS, DP), F32),
        ((ROWS, DP), BF),
        ((ROWS, 2 * FF), BF),
        ((ROWS, FF), BF),
        ((ROWS, DP), F32),
        ((ROWS, DP), F32),
        ((ROWS, DP), F32),
        ((ROWS, DP), BF),
        ((ROWS, DP), BF),
        ((ROWS, 640), F32),
        ((8, DP), F32),
        ((8, DP), F32),
    ]
    scratch = [pltpu.VMEM(shape, kind) for shape, kind in scratch]
    scratch += [
        pltpu.SemaphoreType.DMA((SEMS,)),
        pltpu.SemaphoreType.DMA((2,)),
        pltpu.SemaphoreType.DMA((2,)),
        pltpu.SemaphoreType.REGULAR,
    ]
    scratch += [pltpu.VMEM(shape, BF) for shape in LANDS]
    vmem = pl.BlockSpec(memory_space=pltpu.VMEM)
    made = pl.pallas_call(
        kernel,
        out_shape=(
            jax.ShapeDtypeStruct((MICRO, D, SEQ), F32),
            *(
                jax.ShapeDtypeStruct((SHARD, 1, width), F32)
                for width in (D, 320, 320, D, FF, FF, FF)
            ),
            jax.ShapeDtypeStruct((1, SHARD), F32),
            jax.ShapeDtypeStruct((1, SHARD), F32),
        ),
        in_specs=[vmem] * 10 + [pl.BlockSpec(memory_space=pltpu.SMEM), vmem, vmem],
        out_specs=(vmem,) * 10,
        scratch_shapes=scratch,
        compiler_params=pltpu.CompilerParams(
            collective_id=0, has_side_effects=True, vmem_limit_bytes=64 * 1024 * 1024
        ),
    )(*weights, gain_attn, gain_mlp, rows_in, lengths, cosine, sine)
    count = len(made)
    return pl.pallas_call(
        hand_on,
        out_shape=tuple(jax.ShapeDtypeStruct(one.shape, one.dtype) for one in made),
        in_specs=[vmem] * count,
        out_specs=(vmem,) * count,
    )(*made)


def local(
    boundary, lengths, gain_attn, w_query, w_key, w_value, w_out, gain_mlp, w_gate, w_up, w_down
):
    cosine, sine = rope_tables()
    weights = (w_query[0], w_out[0].T, w_key[0], w_value[0], w_gate[0], w_up[0], w_down[0].T)
    ends, query, key, value, out, gate, up, down, gain_one, gain_two = run_kernel(
        weights,
        gain_attn,
        gain_mlp,
        boundary[0].transpose(0, 2, 1),
        lengths.T,
        jnp.asarray(cosine),
        jnp.asarray(sine),
    )

    def rows(grad):
        return grad.transpose(1, 0, 2)

    def turned(grad):
        return grad.transpose(1, 2, 0)

    return (
        ends.transpose(0, 2, 1)[None],
        gain_one,
        rows(query),
        rows(key),
        rows(value),
        turned(out),
        gain_two,
        rows(gate),
        rows(up),
        turned(down),
    )


def solution(mesh):
    row = P("section", "dp", None)
    column = P("section", None, "dp")
    gain = P("section", "dp")
    ends = P("section", None, "dp", None)
    weights = (gain, row, row, row, column, gain, row, row, column)
    return jax.shard_map(
        local,
        mesh=mesh,
        in_specs=(ends, P(None, "dp")) + weights,
        out_specs=(ends,) + weights,
        check_vma=False,
    )
```

```python
import numpy as np

import jax
import jax.numpy as jnp
from jax import lax
from jax.experimental import pallas as pl
from jax.experimental.pallas import tpu as pltpu
from jax.sharding import PartitionSpec as P

D = 960
DP = 1024
HQ = 15
KV = 5
GROUP = HQ // KV
HD = 64
FF = 2560
SEQ = 128
MICRO = 2
ROWS = MICRO * SEQ
RING = 4
SHARD = 15
PADDED = 16
EPS = 1e-05
NEG = -1e30
BASE = 10000.0
BF = jnp.bfloat16
F32 = jnp.float32
MESH = pl.DeviceIdType.MESH

C_Q = 0
C_KV = 1024
C_O = 1664
C_FF = 2688
C_ALL = C_FF + 3 * FF
SUB = 512

STRIDES = (16, 4, 1)
ORDERS = ((0, 1, 2), (1, 2, 0), (2, 0, 1))

CHUNKS = ((0, 1024), (1024, 2048), (2048, 2560))
LARGE = [
    [(0, 512, 896, 0), (896, 1280, 1664, 1)],
    [(1664, 1792, 1792, 1), (1792, 2304, 2688, 2)],
] + [
    [
        (C_FF + FF * part + first, C_FF + FF * part + (first + last) // 2, C_FF + FF * part + last, part)
        for part in range(3)
    ]
    for first, last in CHUNKS
]
GROUPS = len(LARGE)
MERGED = [
    [(896 * part, 896 * part + 512, 896 * part + 896, part) for part in range(3)],
    [
        (C_FF + FF * part, C_FF + FF * part + FF // 2, C_FF + FF * part + FF, part)
        for part in range(3)
    ],
]


def position():
    me = lax.axis_index("dp")
    return me, (me // 16, (me // 4) % 4, me % 4)


def neighbour(me, coords, axis, step):
    here = coords[axis]
    return me + ((here + step) % RING - here) * STRIDES[axis]


def remote(src, dst, send, recv, device):
    return pltpu.make_async_remote_copy(
        src_ref=src,
        dst_ref=dst,
        send_sem=send,
        recv_sem=recv,
        device_id={"dp": device},
        device_id_type=MESH,
    )


class Ring:
    def __init__(self, piece, phase, later_full, whole, sems, me, coords):
        self.first, self.mid, self.last, part = piece
        self.order, self.phase, self.later_full = ORDERS[part], phase, later_full
        self.axis = self.order[phase]
        self.whole, self.sems = whole, sems
        self.me, self.coords = me, coords
        self.near = neighbour(me, coords, self.axis, 1)
        here = coords[self.axis]
        self.here, self.ahead, self.across, self.behind = [
            (here + step) % RING for step in range(4)
        ]

    def span(self, side):
        return ((self.first, self.last), (self.first, self.mid), (self.mid, self.last))[side]

    def view(self, at, side=0):
        first, last = self.span(side)
        index = [None, None, None]
        for place, axis in enumerate(self.order):
            if place == self.phase:
                index[axis] = at
            elif (place > self.phase) == self.later_full:
                index[axis] = slice(None)
            else:
                index[axis] = self.coords[axis]
        return self.whole.at[index[0], index[1], index[2], :, first:last]

    def widths(self):
        return [side for side in (1, 2) if self.span(side)[0] < self.span(side)[1]]

    def copy(self, src, dst, send, recv, step):
        remote(
            src,
            dst,
            self.sems.at[send],
            self.sems.at[recv],
            neighbour(self.me, self.coords, self.axis, step),
        ).start()

    def wait_recv(self, ref, sem):
        remote(ref, ref, self.sems.at[sem], self.sems.at[sem], self.near).wait_recv()

    def wait_send(self, ref, sem):
        remote(ref, ref, self.sems.at[sem], self.sems.at[sem], self.near).wait_send()


class DirectGather(Ring):
    count = 2

    def go(self):
        view = self.view(self.here)
        for step in (1, -1, 2):
            self.copy(view, view, 0, 1, step)

    def done(self):
        self.wait_recv(self.view(slice(0, 3)), 1)

    def finish(self):
        self.wait_send(self.view(slice(0, 3)), 0)


class RingGather(Ring):
    count = 3

    def go(self):
        view = self.view(self.here)
        self.copy(view, view, 0, 1, 1)
        self.copy(view, view, 0, 1, -1)

    def forward(self):
        self.wait_recv(self.view(slice(0, 2)), 1)
        sides = self.widths()
        right = self.view(self.behind, 1)
        self.copy(right, right, 0, 2, 1)
        if 2 in sides:
            left = self.view(self.ahead, 2)
            self.copy(left, left, 0, 2, -1)

    def done(self):
        self.wait_recv(self.view(self.here), 2)

    def finish(self):
        self.wait_send(self.view(slice(0, 3)), 0)


class DirectScatter(Ring):
    count = 2

    def __init__(self, *args, lands, result=None):
        super().__init__(*args)
        (self.land,), self.result = lands, result

    def go(self):
        for slot, step in enumerate((1, -1, 2)):
            at = (self.ahead, self.behind, self.across)[slot]
            self.copy(self.view(at), self.land.at[slot], 0, 1, step)

    def done(self):
        self.wait_recv(self.land, 1)
        view = self.view(self.here)
        if self.result is not None:
            total = view[...].astype(F32)
            for slot in range(3):
                total = total + self.land[slot].astype(F32)
            self.result(self.first, self.last, total)
            return

        def one(step, carry):
            total = view[step].astype(F32)
            for slot in range(3):
                total = total + self.land[slot, step].astype(F32)
            view[step] = total.astype(BF)
            return carry

        lax.fori_loop(0, RING, one, 0)

    def finish(self):
        self.wait_send(self.land, 0)


class RingScatter(Ring):
    count = 6

    def __init__(self, *args, lands):
        super().__init__(*args)
        self.lands = dict(zip(self.widths(), lands))

    def send(self, side, slot, at, step):
        base = 3 * (side - 1)
        self.copy(
            self.view(at, side), self.lands[side].at[slot], base, base + (1 if slot == 0 else 2), step
        )

    def add(self, at, side, slots):
        view, land = self.view(at, side), self.lands[side]

        def one(step, carry):
            total = view[step].astype(F32)
            for slot in slots:
                total = total + land[slot, step].astype(F32)
            view[step] = total.astype(BF)
            return carry

        lax.fori_loop(0, RING, one, 0)

    def go(self):
        sides = self.widths()
        self.send(1, 0, self.across, 1)
        if 2 in sides:
            self.send(2, 0, self.across, -1)
            self.send(2, 1, self.ahead, 1)
        self.send(1, 1, self.behind, -1)

    def forward(self):
        for side in self.widths():
            step, at = ((1, self.ahead), (-1, self.behind))[side - 1]
            self.wait_recv(self.lands[side].at[0], 3 * (side - 1) + 1)
            self.add(at, side, (0,))
            self.send(side, 2, at, step)

    def done(self):
        for side in self.widths():
            self.wait_recv(self.lands[side].at[1:3], 3 * (side - 1) + 2)
            self.add(self.here, side, (1, 2))

    def finish(self):
        for side in self.widths():
            self.wait_send(self.lands[side], 3 * (side - 1))


PLAN = {}
LANDS = []
SEMS = 0
for kind, cls, pieces, phase in (
    ("g1", DirectGather, MERGED, 0),
    ("g2", RingGather, MERGED, 1),
    ("g3", RingGather, LARGE, 2),
    ("s1", RingScatter, LARGE, 0),
    ("s2", DirectScatter, MERGED[:1], 1),
    ("s2", RingScatter, MERGED[1:], 1),
    ("s3", DirectScatter, MERGED, 2),
):
    for group in pieces:
        entries = []
        for piece in group:
            mine = []
            first, mid, last, _ = piece
            if cls is DirectScatter:
                mine = [last - first]
            elif cls is RingScatter:
                mine = [width for width in (mid - first, last - mid) if width]
            for width in mine:
                LANDS.append((3,) + (RING,) * (2 - phase) + (PADDED, width))
            entries.append((cls, piece, phase, SEMS, len(LANDS) - len(mine), len(LANDS)))
            SEMS += cls.count
        PLAN.setdefault(kind, []).append(entries)


def dot(left, right):
    return jnp.dot(left, right, preferred_element_type=F32)


def dot_nt(left, right):
    return lax.dot_general(left, right, (((1,), (1,)), ((), ())), preferred_element_type=F32)


def dot_tn(left, right):
    return lax.dot_general(left, right, (((0,), (0,)), ((), ())), preferred_element_type=F32)


def columns(whole, first, count):
    return whole[:, :, :, :, pl.ds(first, count)].reshape(DP, count)


def swap_halves(tile):
    lane = lax.broadcasted_iota(jnp.int32, tile.shape, 1)
    return jnp.where(lane % HD < HD // 2, pltpu.roll(tile, 96, 1), pltpu.roll(tile, 32, 1))


def norm_forward(matrix, gain):
    scale = lax.rsqrt(jnp.sum(matrix * matrix, axis=1, keepdims=True) * (1.0 / D) + EPS)
    return (matrix * scale * gain).astype(BF)


def norm_backward(matrix, gain, grad):
    scale = lax.rsqrt(jnp.sum(matrix * matrix, axis=1, keepdims=True) * (1.0 / D) + EPS)
    scaled = grad * gain
    inner = jnp.sum(scaled * matrix, axis=1, keepdims=True) * (1.0 / D)
    grad_matrix = scale * (scaled - matrix * (scale * scale * inner))
    grad_gain = jnp.sum(grad * matrix * scale, axis=0, keepdims=True)
    return grad_matrix, grad_gain


def kernel(
    w_query,
    w_out,
    w_key,
    w_value,
    w_gate,
    w_up,
    w_down,
    gain_attn,
    gain_mlp,
    rows_in,
    lengths,
    cosine,
    sine,
    ends,
    grad_w_query,
    grad_w_key,
    grad_w_value,
    grad_w_out,
    grad_w_gate,
    grad_w_up,
    grad_w_down,
    grad_gain_attn,
    grad_gain_mlp,
    whole,
    entering,
    grad_out,
    crossing,
    spread,
    normed_one,
    queries,
    key_value,
    probs,
    mixed,
    resid,
    normed_two,
    gate_up,
    hidden,
    total,
    total_back,
    grad_resid,
    grad_branch,
    grad_mixed,
    grad_kv,
    gains,
    grad_gains,
    sems,
    cross_send,
    cross_recv,
    turn,
    *lands,
):
    section = lax.axis_index("section")
    me, coords = position()
    is_first = section == 0

    barrier = pltpu.get_barrier_semaphore()
    for axis in range(3):
        for step in (1, -1, 2):
            pl.semaphore_signal(
                barrier,
                inc=1,
                device_id={"dp": neighbour(me, coords, axis, step)},
                device_id_type=MESH,
            )
    pl.semaphore_signal(barrier, inc=1, device_id={"section": 1 - section}, device_id_type=MESH)

    unit = jnp.where(
        lax.broadcasted_iota(jnp.int32, (PADDED, SHARD), 0)
        == lax.broadcasted_iota(jnp.int32, (PADDED, SHARD), 1),
        1.0,
        0.0,
    ).astype(BF)
    place = jnp.where(
        lax.broadcasted_iota(jnp.int32, (SHARD, DP), 1)
        == lax.broadcasted_iota(jnp.int32, (SHARD, DP), 0) + me * PADDED,
        1.0,
        0.0,
    ).astype(BF)
    last_row = lax.broadcasted_iota(jnp.int32, (PADDED, DP), 0) == SHARD

    def set_block(first, value):
        whole[coords[0], coords[1], coords[2], :, first : first + value.shape[1]] = value.astype(BF)

    def with_gain(weights, gain):
        body = jnp.concatenate(
            [dot(unit, weights[...]), jnp.zeros((PADDED, DP - D), F32)], axis=1
        )
        return jnp.where(last_row, dot(gain[...], place), body)

    set_block(C_Q, with_gain(w_query, gain_attn))
    set_block(C_O, with_gain(w_out, gain_mlp))
    set_block(C_KV, jnp.concatenate([dot(unit, w_key[...]), dot(unit, w_value[...])], axis=1))
    for part, weights in enumerate((w_gate, w_up, w_down)):
        set_block(C_FF + FF * part, dot(unit, weights[...]))
    pl.semaphore_wait(barrier, 10)

    homes = (
        (C_Q, D, grad_w_query),
        (C_KV, 320, grad_w_key),
        (C_KV + 320, 320, grad_w_value),
        (C_O, D, grad_w_out),
        (C_FF, FF, grad_w_gate),
        (C_FF + FF, FF, grad_w_up),
        (C_FF + 2 * FF, FF, grad_w_down),
    )

    def put_result(first, last, value):
        for start, count, ref in homes:
            low, high = max(first, start), min(last, start + count)
            if low < high:
                for row in range(SHARD):
                    ref[row, :, low - start : high - start] = value[
                        row : row + 1, low - first : high - first
                    ]
        for slot, start in enumerate((C_Q, C_O)):
            low, high = max(first, start), min(last, start + DP)
            if low < high:
                grad_gains[2 + slot : 3 + slot, low - start : high - start] = value[
                    SHARD : SHARD + 1, low - first : high - first
                ]

    started = []

    def make(entry):
        cls, piece, phase, sem, land, land_end = entry
        args = (piece, phase, cls in (RingScatter, DirectScatter), whole)
        args += (sems.at[sem : sem + cls.count], me, coords)
        if cls is DirectScatter:
            made = cls(
                *args, lands=lands[land:land_end], result=put_result if phase == 2 else None
            )
        elif cls is RingScatter:
            made = cls(*args, lands=lands[land:land_end])
        else:
            made = cls(*args)
        started.append(made)
        return made

    transfers = {
        kind: [[make(entry) for entry in group] for group in groups]
        for kind, groups in PLAN.items()
    }
    scatters = [made for made in started if isinstance(made, (DirectScatter, RingScatter))]

    def run(kind, group, act):
        for made in transfers[kind][group]:
            getattr(made, act)()

    run("g1", 0, "go")
    run("g1", 1, "go")

    row = lax.broadcasted_iota(jnp.int32, (D, DP), 0)
    column = lax.broadcasted_iota(jnp.int32, (D, DP), 1)
    chosen = (column - column // PADDED == row) & (column % PADDED != SHARD)
    spread[...] = jnp.where(chosen, 1.0, 0.0).astype(BF)
    own_rows = jnp.concatenate(
        [dot_tn(rows_in[micro], spread[...]) for micro in range(MICRO)], axis=0
    ).astype(BF)

    @pl.when(is_first)
    def _():
        entering[...] = own_rows

    @pl.when(jnp.logical_not(is_first))
    def _():
        grad_out[...] = own_rows

    for group in range(2):
        run("g1", group, "done")
        run("g2", group, "go")

    def hand_over():
        @pl.when(is_first)
        def _():
            pl.semaphore_signal(
                turn, inc=1, device_id={"section": 1 - section}, device_id_type=MESH
            )

    def take_over():
        @pl.when(jnp.logical_not(is_first))
        def _():
            pl.semaphore_wait(turn, 1)

    for group in range(2):
        run("g2", group, "forward")
    run("g2", 0, "done")
    take_over()
    run("g3", 0, "go")
    run("g3", 1, "go")
    run("g2", 1, "done")
    run("g3", 2, "go")
    run("g3", 0, "forward")
    run("g3", 3, "go")
    run("g3", 1, "forward")
    run("g3", 4, "go")
    run("g3", 2, "forward")
    run("g3", 0, "done")

    def cross(target, slot):
        return pltpu.make_async_remote_copy(
            src_ref=crossing,
            dst_ref=target,
            send_sem=cross_send.at[slot],
            recv_sem=cross_recv.at[slot],
            device_id={"section": 1 - section},
            device_id_type=MESH,
        )

    middle_copy = cross(entering, 0)
    grad_copy = cross(grad_out, 1)

    picks = jnp.where(
        lax.broadcasted_iota(jnp.int32, (PADDED, DP), 1) % PADDED == SHARD, 1.0, 0.0
    ).astype(BF)
    gains[0:1, :] = dot(picks, columns(whole, C_Q, DP))[0:1]

    @pl.when(jnp.logical_not(is_first))
    def _():
        middle_copy.wait_recv()

    normed_one[...] = norm_forward(entering[...].astype(F32), gains[0:1, :])

    cos_rows = jnp.concatenate([cosine[...]] * MICRO, axis=0)
    sin_rows = jnp.concatenate([sine[...]] * MICRO, axis=0)
    low_lane = lax.broadcasted_iota(jnp.int32, (ROWS, 128), 1) < HD

    for half in range(2):
        pre = dot(normed_one[...], columns(whole, C_Q + half * 512, 512))
        for tile in range(4):
            part = pre[:, tile * 128 : tile * 128 + 128]
            at = half * 512 + tile * 128
            queries[:, at : at + 128] = (part * cos_rows + swap_halves(part) * sin_rows).astype(BF)
    pre = dot(normed_one[...], columns(whole, C_KV, 640))
    for tile in range(5):
        part = pre[:, tile * 128 : tile * 128 + 128]
        if tile < 3:
            turned = part * cos_rows + swap_halves(part) * sin_rows
            part = turned if tile < 2 else jnp.where(low_lane, turned, part)
        key_value[:, tile * 128 : tile * 128 + 128] = part.astype(BF)

    def attend(seq, carry):
        rows = pl.ds(pl.multiple_of(seq * SEQ, SEQ), SEQ)
        query_pos = lax.broadcasted_iota(jnp.int32, (GROUP, SEQ, SEQ), 1).reshape(GROUP * SEQ, SEQ)
        key_pos = lax.broadcasted_iota(jnp.int32, (GROUP * SEQ, SEQ), 1)
        allowed = (key_pos <= query_pos) & (key_pos < lengths[0, seq])
        query_rows = queries[rows, :]
        kv_rows = key_value[rows, :]
        heads = []
        for group in range(KV):
            at = group * GROUP * HD
            query = jnp.concatenate(
                [query_rows[:, at + h * HD : at + h * HD + HD] for h in range(GROUP)], axis=0
            )
            key = kv_rows[:, group * HD : group * HD + HD]
            value = kv_rows[:, (KV + group) * HD : (KV + group) * HD + HD]
            scores = jnp.where(allowed, dot_nt(query, key) * HD**-0.5, NEG)
            expos = jnp.exp(scores - jnp.max(scores, axis=1, keepdims=True))
            chances = expos / jnp.sum(expos, axis=1, keepdims=True)
            probs[seq, group] = chances
            out = dot(chances.astype(BF), value)
            heads.extend(out[h * SEQ : h * SEQ + SEQ] for h in range(GROUP))
        heads.append(jnp.zeros((SEQ, HD), F32))
        mixed[rows, :] = jnp.concatenate(heads, axis=1).astype(BF)
        return carry

    lax.fori_loop(0, MICRO, attend, 0)
    run("g3", 3, "forward")
    run("g3", 1, "done")
    gains[1:2, :] = dot(picks, columns(whole, C_O, DP))[0:1]
    inside = lax.broadcasted_iota(jnp.int32, (ROWS, DP), 1) % PADDED != SHARD
    branch = jnp.where(inside, dot_nt(mixed[...], columns(whole, C_O, DP)), 0.0)
    matrix = entering[...].astype(F32) + branch
    resid[...] = matrix
    normed_two[...] = norm_forward(matrix, gains[1:2, :])
    total[...] = matrix
    run("g3", 4, "forward")
    hand_over()

    def feed(chunk):
        def one(step, carry):
            unit_at = pl.multiple_of(step * SUB, SUB)
            gates = dot(normed_two[...], columns(whole, C_FF + unit_at, SUB))
            uppers = dot(normed_two[...], columns(whole, C_FF + FF + unit_at, SUB))
            gate_up[:, pl.ds(unit_at, SUB)] = gates.astype(BF)
            gate_up[:, pl.ds(FF + unit_at, SUB)] = uppers.astype(BF)
            hiddens = (gates / (1.0 + jnp.exp(-gates)) * uppers).astype(BF)
            hidden[:, pl.ds(unit_at, SUB)] = hiddens
            total[...] += dot_nt(hiddens, columns(whole, C_FF + 2 * FF + unit_at, SUB))
            return carry

        first, last = CHUNKS[chunk]
        lax.fori_loop(first // SUB, last // SUB, one, 0)

    def put(left, right, first, count, gain=None):
        grad = dot_tn(left, right)
        if gain is not None:
            at, gain_row = gain
            row = lax.broadcasted_iota(jnp.int32, (DP, count), 0)
            column = lax.broadcasted_iota(jnp.int32, (DP, count), 1) + at
            own = (row % PADDED == SHARD) & (row // PADDED == column // PADDED)
            grad = jnp.where(own, gain_row, grad)
        whole[:, :, :, :, pl.ds(first, count)] = grad.astype(BF).reshape(4, 4, 4, PADDED, count)

    def feed_back(chunk):
        def one(step, carry):
            unit_at = pl.multiple_of(step * SUB, SUB)
            gate_at, up_at, down_at = [C_FF + FF * part + unit_at for part in range(3)]
            grad_hidden = dot(grad_out[...], columns(whole, down_at, SUB))
            gates = gate_up[:, pl.ds(unit_at, SUB)].astype(F32)
            uppers = gate_up[:, pl.ds(FF + unit_at, SUB)].astype(F32)
            opened = 1.0 / (1.0 + jnp.exp(-gates))
            slope = opened * (1.0 + gates * (1.0 - opened))
            grad_gate = (grad_hidden * uppers * slope).astype(BF)
            grad_up = (grad_hidden * (gates * opened)).astype(BF)
            total_back[...] += dot_nt(grad_gate, columns(whole, gate_at, SUB)) + dot_nt(
                grad_up, columns(whole, up_at, SUB)
            )
            put(normed_two[...], grad_gate, gate_at, SUB)
            put(normed_two[...], grad_up, up_at, SUB)
            put(grad_out[...], hidden[:, pl.ds(unit_at, SUB)], down_at, SUB)
            return carry

        first, last = CHUNKS[chunk]
        lax.fori_loop(first // SUB, last // SUB, one, 0)

    def turn_back(chunk):
        feed_back(chunk)
        run("s1", chunk + 2, "go")

    total_back[...] = jnp.zeros_like(total_back)
    run("g1", 1, "finish")
    run("g2", 1, "finish")
    for chunk in range(len(CHUNKS)):
        run("g3", chunk + 2, "done")
        run("g3", chunk + 2, "finish")
        feed(chunk)

        @pl.when(jnp.logical_not(is_first))
        def _():
            turn_back(chunk)


    def put_ends(value):
        high = value.astype(BF)
        low = (value - high.astype(F32)).astype(BF)
        for micro in range(MICRO):
            rows = slice(micro * SEQ, micro * SEQ + SEQ)
            ends[micro] = dot_nt(spread[...], high[rows]) + dot_nt(spread[...], low[rows])

    @pl.when(is_first)
    def _():
        crossing[...] = total[...].astype(BF)
        middle_copy.start()

    for kind, group in (("g1", 0), ("g2", 0), ("g3", 0), ("g3", 1)):
        run(kind, group, "finish")

    @pl.when(is_first)
    def _():
        middle_copy.wait_send()
        grad_copy.wait_recv()

    @pl.when(is_first)
    def _():
        for chunk in range(len(CHUNKS)):
            turn_back(chunk)

    through, grad_gain = norm_backward(resid[...], gains[1:2, :], total_back[...])
    grad_gains[1:2, :] = grad_gain
    through = through + grad_out[...].astype(F32)
    grad_resid[...] = through
    grad_branch[...] = through.astype(BF)
    grad_mixed[...] = dot(grad_branch[...], columns(whole, C_O, DP)).astype(BF)
    for half in range(2):
        at = half * SUB
        here = slice(at, at + SUB)
        put(grad_branch[...], mixed[:, here], C_O + at, SUB, (at, grad_gains[1:2, here]))
    run("s1", 1, "go")

    @pl.when(jnp.logical_not(is_first))
    def _():
        run("s1", 2, "forward")


    def attend_back(seq, carry):
        rows = pl.ds(pl.multiple_of(seq * SEQ, SEQ), SEQ)
        query_rows = queries[rows, :]
        kv_rows = key_value[rows, :]
        grad_rows = grad_mixed[rows, :]
        query_parts = []
        key_parts = []
        value_parts = []
        for group in range(KV):
            at = group * GROUP * HD
            query = jnp.concatenate(
                [query_rows[:, at + h * HD : at + h * HD + HD] for h in range(GROUP)], axis=0
            )
            grad = jnp.concatenate(
                [grad_rows[:, at + h * HD : at + h * HD + HD] for h in range(GROUP)], axis=0
            )
            key = kv_rows[:, group * HD : group * HD + HD]
            value = kv_rows[:, (KV + group) * HD : (KV + group) * HD + HD]
            chances = probs[seq, group]
            grad_probs = dot_nt(grad, value)
            inner = jnp.sum(chances * grad_probs, axis=1, keepdims=True)
            grad_scores = (chances * (grad_probs - inner)).astype(BF)
            grad_query = dot(grad_scores, key) * HD**-0.5
            query_parts.extend(grad_query[h * SEQ : h * SEQ + SEQ] for h in range(GROUP))
            key_parts.append(dot_tn(grad_scores, query) * HD**-0.5)
            value_parts.append(dot_tn(chances.astype(BF), grad))
        query_parts.append(jnp.zeros((SEQ, HD), F32))
        total_back[rows, :] = jnp.concatenate(query_parts, axis=1)
        grad_kv[rows, :] = jnp.concatenate(key_parts + value_parts, axis=1)
        return carry

    lax.fori_loop(0, MICRO, attend_back, 0)

    @pl.when(jnp.logical_not(is_first))
    def _():
        run("s1", 3, "forward")

    grad_query = grad_mixed
    for tile in range(8):
        part = total_back[:, tile * 128 : tile * 128 + 128]
        grad_query[:, tile * 128 : tile * 128 + 128] = (
            part * cos_rows - swap_halves(part) * sin_rows
        ).astype(BF)
    for tile in range(5):
        part = grad_kv[:, tile * 128 : tile * 128 + 128]
        if tile < 3:
            turned = part * cos_rows - swap_halves(part) * sin_rows
            part = turned if tile < 2 else jnp.where(low_lane, turned, part)
        key_value[:, tile * 128 : tile * 128 + 128] = part.astype(BF)
    grad_normed = dot_nt(grad_query[...], columns(whole, C_Q, DP)) + dot_nt(
        key_value[...], columns(whole, C_KV, 640)
    )
    through, grad_gain = norm_backward(entering[...].astype(F32), gains[0:1, :], grad_normed)
    grad_gains[0:1, :] = grad_gain
    through = through + grad_resid[...]

    @pl.when(is_first)
    def _():
        total[...] = through

    @pl.when(jnp.logical_not(is_first))
    def _():
        crossing[...] = through.astype(BF)
        grad_copy.start()

    for half in range(2):
        at = half * SUB
        here = slice(at, at + SUB)
        put(normed_one[...], grad_query[:, here], C_Q + at, SUB, (at, grad_gains[0:1, here]))
    put(normed_one[...], key_value[...], C_KV, 640)
    run("s1", 0, "go")

    @pl.when(is_first)
    def _():
        run("s1", 2, "forward")
        run("s1", 3, "forward")

    run("s1", 4, "forward")
    run("s1", 1, "forward")
    run("s1", 0, "forward")
    put_ends(total[...])
    for group in (2, 3, 4):
        run("s1", group, "done")
    run("s2", 1, "go")
    run("s1", 1, "done")
    run("s1", 0, "done")
    run("s2", 0, "go")
    run("s2", 1, "forward")
    run("s2", 0, "done")
    run("s3", 0, "go")
    run("s2", 1, "done")
    run("s3", 1, "go")
    run("s3", 0, "done")
    run("s3", 1, "done")
    for slot, gain_result in enumerate((grad_gain_attn, grad_gain_mlp)):
        moved = pltpu.roll(grad_gains[2 + slot : 3 + slot, :], DP - me * PADDED, 1)
        gain_result[...] = moved[:, 0:SHARD]

    @pl.when(jnp.logical_not(is_first))
    def _():
        grad_copy.wait_send()

    for made in scatters:
        made.finish()


def rope_tables():
    frequency = BASE ** (-(np.arange(HD // 2, dtype=np.float32) * np.float32(2.0 / HD)))
    angles = np.arange(SEQ, dtype=np.float32)[:, None] * frequency[None, :].astype(np.float32)
    cos, sin = np.cos(angles), np.sin(angles)
    return (
        np.concatenate([cos, cos, cos, cos], axis=1).astype(np.float32),
        np.concatenate([-sin, sin, -sin, sin], axis=1).astype(np.float32),
    )


def hand_on(*refs):
    count = len(refs) // 2
    for source, target in zip(refs[:count], refs[count:]):
        target[...] = source[...]


def run_kernel(weights, gain_attn, gain_mlp, rows_in, lengths, cosine, sine):
    scratch = [
        ((RING, RING, RING, PADDED, C_ALL), BF),
        ((ROWS, DP), BF),
        ((ROWS, DP), BF),
        ((ROWS, DP), BF),
        ((D, DP), BF),
        ((ROWS, DP), BF),
        ((ROWS, DP), BF),
        ((ROWS, 640), BF),
        ((MICRO, KV, GROUP * SEQ, SEQ), F32),
        ((ROWS, DP), BF),
        ((ROWS, DP), F32),
        ((ROWS, DP), BF),
        ((ROWS, 2 * FF), BF),
        ((ROWS, FF), BF),
        ((ROWS, DP), F32),
        ((ROWS, DP), F32),
        ((ROWS, DP), F32),
        ((ROWS, DP), BF),
        ((ROWS, DP), BF),
        ((ROWS, 640), F32),
        ((8, DP), F32),
        ((8, DP), F32),
    ]
    scratch = [pltpu.VMEM(shape, kind) for shape, kind in scratch]
    scratch += [
        pltpu.SemaphoreType.DMA((SEMS,)),
        pltpu.SemaphoreType.DMA((2,)),
        pltpu.SemaphoreType.DMA((2,)),
        pltpu.SemaphoreType.REGULAR,
    ]
    scratch += [pltpu.VMEM(shape, BF) for shape in LANDS]
    vmem = pl.BlockSpec(memory_space=pltpu.VMEM)
    made = pl.pallas_call(
        kernel,
        out_shape=(
            jax.ShapeDtypeStruct((MICRO, D, SEQ), F32),
            *(
                jax.ShapeDtypeStruct((SHARD, 1, width), F32)
                for width in (D, 320, 320, D, FF, FF, FF)
            ),
            jax.ShapeDtypeStruct((1, SHARD), F32),
            jax.ShapeDtypeStruct((1, SHARD), F32),
        ),
        in_specs=[vmem] * 10 + [pl.BlockSpec(memory_space=pltpu.SMEM), vmem, vmem],
        out_specs=(vmem,) * 10,
        scratch_shapes=scratch,
        compiler_params=pltpu.CompilerParams(
            collective_id=0, has_side_effects=True, vmem_limit_bytes=64 * 1024 * 1024
        ),
    )(*weights, gain_attn, gain_mlp, rows_in, lengths, cosine, sine)
    count = len(made)
    return pl.pallas_call(
        hand_on,
        out_shape=tuple(jax.ShapeDtypeStruct(one.shape, one.dtype) for one in made),
        in_specs=[vmem] * count,
        out_specs=(vmem,) * count,
    )(*made)


def local(
    boundary, lengths, gain_attn, w_query, w_key, w_value, w_out, gain_mlp, w_gate, w_up, w_down
):
    cosine, sine = rope_tables()
    weights = (w_query[0], w_out[0].T, w_key[0], w_value[0], w_gate[0], w_up[0], w_down[0].T)
    ends, query, key, value, out, gate, up, down, gain_one, gain_two = run_kernel(
        weights,
        gain_attn,
        gain_mlp,
        boundary[0].transpose(0, 2, 1),
        lengths.T,
        jnp.asarray(cosine),
        jnp.asarray(sine),
    )

    def rows(grad):
        return grad.transpose(1, 0, 2)

    def turned(grad):
        return grad.transpose(1, 2, 0)

    return (
        ends.transpose(0, 2, 1)[None],
        gain_one,
        rows(query),
        rows(key),
        rows(value),
        turned(out),
        gain_two,
        rows(gate),
        rows(up),
        turned(down),
    )


def solution(mesh):
    row = P("section", "dp", None)
    column = P("section", None, "dp")
    gain = P("section", "dp")
    ends = P("section", None, "dp", None)
    weights = (gain, row, row, row, column, gain, row, row, column)
    return jax.shard_map(
        local,
        mesh=mesh,
        in_specs=(ends, P(None, "dp")) + weights,
        out_specs=(ends,) + weights,
        check_vma=False,
    )
```
